32 devices in a mesh: dp: 8 (over z, x), sp: 4 (over y, core).
Axes of the slice: x: 2, y: 2, z: 4, core: 2. Of those that a mesh axis runs over, the one named last changes fastest.
Arguments:
- base_query: bfloat16 [8, 1024, 4096], P('dp', 'sp'), may hold values from -8 to 8
- base_key: bfloat16 [8, 1024, 512], P('dp', 'sp'), may hold values from -8 to 8
- reference_value_rows: bfloat16 [8, 1024, 512], P('dp', 'sp'), may hold values from -6 to 6
- actor_query: bfloat16 [8, 1024, 4096], P('dp', 'sp'), may hold values from -8 to 8
- actor_key: bfloat16 [8, 1024, 512], P('dp', 'sp'), may hold values from -8 to 8
- actor_value_rows: bfloat16 [8, 1024, 512], P('dp', 'sp'), may hold values from -6 to 6
- segment_labels: int32 [8, 1024], P('dp', 'sp'), may hold values from 0 to 2, never falling along the last dimension, each value on 1 to 512 neighbouring positions
- shard_plan: int32 [8], replicated, may hold values from 0 to 7, each once
Outputs:
- base_output: bfloat16 [8, 1024, 4096], P('dp', 'sp')
- actor_output: bfloat16 [8, 1024, 4096], P('dp', 'sp')
The draws below stay inside these ranges and needn't reach their ends.
Inputs may be any that keep to these rules, and one draw needn't show every extreme that they name: `segment_labels`: along an owner's rows the labels never decrease; a response has 1 to 512 rows, and some response has exactly 512. `shard_plan`: each group is named by exactly one owner.
All inputs are finite; a program needn't handle non-finite values.
Results may differ from the reference program's by a relative error of at most 0.0079.
Values may be sent and summed in bfloat16 or wider, within the bound.
A program may use at most 128 MiB of HBM per device.

```python
import math
import jax
import jax.numpy as jnp
import numpy as np
from jax import lax

QUERY_HEADS = 32
KEY_VALUE_HEADS = 4
HEAD_SIZE = 128
SEGS = 3
OWNER_COUNT = 8
OWNER_ROWS = 1024


def drawn_normal(key, head_count):
    return jnp.clip(jax.random.normal(key, (OWNER_COUNT, OWNER_ROWS, head_count * HEAD_SIZE), dtype=jnp.float32), -6.0, 6.0)


def draw_base_query(key, part):
    key = jax.random.fold_in(key, 11)
    return drawn_normal(key, QUERY_HEADS).astype(jnp.bfloat16)


def draw_base_key(key, part):
    key = jax.random.fold_in(key, 12)
    return drawn_normal(key, KEY_VALUE_HEADS).astype(jnp.bfloat16)


def draw_actor_query(key, part):
    key = jax.random.fold_in(key, 13)
    return drawn_normal(key, QUERY_HEADS).astype(jnp.bfloat16)


def draw_actor_key(key, part):
    key = jax.random.fold_in(key, 14)
    return drawn_normal(key, KEY_VALUE_HEADS).astype(jnp.bfloat16)


def steps_of(key, shape, shards, smallest, top_value):
    def one(dim, shards_of):
        steps = jax.random.uniform(jax.random.fold_in(jax.random.fold_in(key, 6), dim), (shards_of,), jnp.float32, smallest / len(shards), top_value / len(shards))
        return jnp.repeat(jnp.exp(steps), shape[dim] // shards_of).reshape((-1,) + (1,) * (len(shape) - dim - 1))

    factor_of = one(*shards[0])
    for cut in shards[1:]:
        factor_of = factor_of * one(*cut)
    return factor_of


def length_profile(number_of, total, reach, slope):
    weights = [(1 << 20) // math.isqrt(rank ** slope) + 1 for rank in range(2, number_of + 1)]
    surplus, given = total - reach - (number_of - 1), [1] * (number_of - 1)
    while surplus > 0:
        movable = [i for i in range(number_of - 1) if given[i] < reach]
        pool, left = sum([weights[i] for i in movable]), surplus
        for i in movable:
            extra = min(reach - given[i], max(1, left * weights[i] // pool), surplus)
            given[i] = given[i] + extra
            surplus = surplus - extra
    return np.array([reach] + given)


def uneven(rng, amount, total, reach, lean):
    if amount == 2:
        one = jax.random.randint(rng, (), max(1, total - reach), min(reach, total - 1) + 1)
        return jnp.stack([one, total - one])
    sizes = jnp.asarray(length_profile(amount, total, reach, lean), jnp.int32)
    couples = (amount - 1) // 2
    donor, taker = sizes[1:1 + 2 * couples:2], sizes[2:2 + 2 * couples:2]
    margin = jnp.minimum(donor - 1, reach - taker)
    passed = jax.random.randint(jax.random.fold_in(rng, 1), (couples,), 0, 1 << 20) % (margin + 1)
    sizes = sizes.at[1:1 + 2 * couples:2].set(donor - passed).at[2:2 + 2 * couples:2].set(taker + passed)
    return sizes[jax.random.permutation(jax.random.fold_in(rng, 2), amount)]


def noise(key, shape, width, limit, cuts=(), kind=jnp.bfloat16):
    drawn = jax.random.normal(key, shape, jnp.float32) * width
    if len(cuts) > 0:
        drawn = steps_of(key, shape, cuts, -0.22, 0.18) * drawn
    return jnp.clip(drawn, min=-limit, max=limit).astype(kind)


def setup_inputs(seed: int = 0) -> dict:
    streams_of = jax.random.split(jax.random.key(seed), 9)
    base_query = draw_base_query(jax.random.fold_in(streams_of[8], 71), 0)
    base_key = draw_base_key(jax.random.fold_in(streams_of[8], 71), 0)
    reference_value_rows = noise(streams_of[2], (OWNER_COUNT, OWNER_ROWS, KEY_VALUE_HEADS * HEAD_SIZE), 1.0, 6.0, ((0, 8), (1, 4)))
    actor_query = draw_actor_query(jax.random.fold_in(streams_of[8], 71), 0)
    actor_key = draw_actor_key(jax.random.fold_in(streams_of[8], 71), 0)
    actor_value_rows = noise(streams_of[5], (OWNER_COUNT, OWNER_ROWS, KEY_VALUE_HEADS * HEAD_SIZE), 1.0, 6.0, ((0, 8), (1, 4)))
    segment_labels = jax.vmap(lambda own: jnp.searchsorted(jnp.cumsum(uneven(own, SEGS, OWNER_ROWS, OWNER_ROWS // 2, 2)), jnp.arange(OWNER_ROWS), side="right"))(jax.random.split(streams_of[6], OWNER_COUNT)).reshape((OWNER_COUNT, OWNER_ROWS)).astype(jnp.int32)
    shard_plan = jax.random.permutation(streams_of[7], OWNER_COUNT).astype(jnp.int32)
    return dict(base_query=base_query, base_key=base_key, reference_value_rows=reference_value_rows, actor_query=actor_query, actor_key=actor_key, actor_value_rows=actor_value_rows, segment_labels=segment_labels, shard_plan=shard_plan)


theta_base = 1000000.0

def response_places(labels):
    column_height = labels.shape[0]
    segment_ids = jnp.arange(SEGS).astype(jnp.int32)
    member_table = (labels[:, None] == segment_ids[None, :]).astype(jnp.int32)
    sizes = lax.optimization_barrier(jnp.sum(member_table, axis=0))
    starts = jnp.cumsum(sizes) - sizes
    row_start = lax.optimization_barrier(jnp.sum(member_table * starts[None, :], axis=1))
    return (jnp.arange(column_height).astype(jnp.int32) - row_start).astype(jnp.float32)

def apply_rotary(value_tensor, head_count, head_width, row_positions):
    column_height = value_tensor.shape[0]
    half_width = head_width // 2
    rate_table = jnp.exp(jnp.arange(half_width).astype(jnp.float32) * (-2.0 * math.log(theta_base) / head_width))
    angles = row_positions[:, None] * rate_table[None, :]
    cosine = jnp.cos(angles)[:, None, :]
    sine_part = jnp.sin(angles)[:, None, :]
    shaped = value_tensor.astype(jnp.float32).reshape(column_height, head_count, head_width)
    leading = shaped[:, :, :half_width]
    trailing = shaped[:, :, half_width:]
    turned = jnp.concatenate([leading * cosine - trailing * sine_part, trailing * cosine + leading * sine_part], axis=-1)
    return turned.reshape(column_height, head_count * head_width).astype(jnp.bfloat16)

def attend(queries, key_tensor, value_tensor, labels):
    column_height = queries.shape[0]
    group_span_width = QUERY_HEADS // KEY_VALUE_HEADS
    rows_per_block = min(512, column_height)
    heads_of_keys = key_tensor.astype(jnp.float32).reshape(column_height, KEY_VALUE_HEADS, HEAD_SIZE)
    heads_of_values = value_tensor.astype(jnp.float32).reshape(column_height, KEY_VALUE_HEADS, HEAD_SIZE)
    key_places = jnp.arange(column_height).astype(jnp.int32)
    scaling = 1.0 / math.sqrt(HEAD_SIZE)

    def one_block(block_index):
        start_row = (block_index * rows_per_block).astype(jnp.int32)
        block_of_queries = lax.dynamic_slice_in_dim(queries, start_row, rows_per_block, 0).astype(jnp.float32)
        block_of_queries = block_of_queries.reshape(rows_per_block, KEY_VALUE_HEADS, group_span_width, HEAD_SIZE)
        label_block = lax.dynamic_slice_in_dim(labels, start_row, rows_per_block, 0)
        scores = jnp.einsum('qhgd,khd->hgqk', block_of_queries, heads_of_keys) * scaling
        query_places = start_row + jnp.arange(rows_per_block).astype(jnp.int32)
        allowed = (label_block[:, None] == labels[None, :]) & (key_places[None, :] <= query_places[:, None])
        scores = jnp.where(allowed, scores, -jnp.inf)
        row_peak = lax.optimization_barrier(jnp.max(scores, axis=-1, keepdims=True))
        raised = jnp.exp(scores - row_peak)
        totals = lax.optimization_barrier(jnp.sum(raised, axis=-1, keepdims=True))
        weights = (raised / totals).astype(jnp.bfloat16)
        blended = jnp.einsum('hgqk,khd->qhgd', weights.astype(jnp.float32), heads_of_values)
        return blended.reshape(rows_per_block, QUERY_HEADS * HEAD_SIZE).astype(jnp.bfloat16)
    blocks = lax.map(one_block, jnp.arange(column_height // rows_per_block).astype(jnp.int32))
    return blocks.reshape(column_height, QUERY_HEADS * HEAD_SIZE)

def reference(base_query, base_key, reference_value_rows, actor_query, actor_key, actor_value_rows, segment_labels, shard_plan):

    def policy_pass(queries, key_tensor, value_tensor):

        def one_owner(inputs):
            owner_queries, keys_per_owner, owner_values, owner_labels = inputs
            row_positions = response_places(owner_labels)
            turned_queries = apply_rotary(owner_queries, QUERY_HEADS, HEAD_SIZE, row_positions)
            keys_after_rotary = apply_rotary(keys_per_owner, KEY_VALUE_HEADS, HEAD_SIZE, row_positions)
            return attend(turned_queries, keys_after_rotary, owner_values, owner_labels)
        return lax.map(one_owner, (queries, key_tensor, value_tensor, segment_labels))
    base_output = policy_pass(base_query, base_key, reference_value_rows)
    actor_home = policy_pass(actor_query, actor_key, actor_value_rows)
    owner_index = jnp.arange(OWNER_COUNT).astype(jnp.int32)
    source_owner = lax.optimization_barrier(jnp.sum(owner_index[:, None] * (shard_plan[:, None] == owner_index[None, :]).astype(jnp.int32), axis=0))
    actor_output = jnp.take(actor_home, source_owner, axis=0)
    return (base_output, actor_output)
```

```python
import functools
import math

import jax
import jax.numpy as jnp
import numpy as np
from jax import lax
from jax.experimental import pallas as pl
from jax.experimental.pallas import tpu as pltpu
from jax.sharding import PartitionSpec as P

QUERY_HEADS = 32
KEY_VALUE_HEADS = 4
HEAD_SIZE = 128
GROUP = QUERY_HEADS // KEY_VALUE_HEADS
THETA = 1000000.0
MESH = pl.DeviceIdType.MESH
BF16 = jnp.bfloat16
F32 = jnp.float32


def kernel(
    owners, members, rows, tile,
    plan_ref, lab_ref, rate_ref, bq_ref, bk_ref, bv_ref, aq_ref, ak_ref, av_ref,
    base_out, actor_out,
    labs, cs, sn, bias, kx, vx, att, land, fwd, bo,
    lab_send, lab_recv, k_send, v_send, k_recv, v_recv,
    one_send, one_recv, two_send, two_recv, bo_sem,
):
    D = HEAD_SIZE
    me = lax.axis_index("dp")
    s = lax.axis_index("sp")
    back = 2 * rows
    span = 3 * rows
    splits = owners // GROUP
    part = rows // splits

    def col(h):
        return pl.ds(pl.multiple_of(h * D, D), D)

    labs[2] = jnp.broadcast_to(lab_ref[...], labs.shape[1:])
    barrier = pltpu.get_barrier_semaphore()

    def greet_owner(j, c):
        pl.semaphore_signal(
            barrier, inc=1, device_id={"dp": lax.rem(me + j, owners)}, device_id_type=MESH
        )
        return c

    lax.fori_loop(1, owners, greet_owner, 0)
    for j in range(1, members):
        pl.semaphore_signal(
            barrier, inc=1, device_id={"sp": lax.rem(s + j, members)}, device_id_type=MESH
        )
    pl.semaphore_wait(barrier, owners - 1 + members - 1)

    def to_later(src, dst_of, send_sem, recv_sem):
        for step in (1, 2):
            pltpu.make_async_remote_copy(
                src_ref=src,
                dst_ref=dst_of(2 - step),
                send_sem=send_sem,
                recv_sem=recv_sem,
                device_id={"sp": lax.rem(s + step, members)},
                device_id_type=MESH,
            ).start()

    def send_key(p, h):
        to_later(
            kx.at[p, pl.ds(back, rows), col(h)],
            lambda slot: kx.at[p, pl.ds(slot * rows, rows), col(h)],
            k_send.at[p], k_recv.at[p, h],
        )

    def send_value(p, v_ref, h):
        to_later(
            v_ref.at[:, col(h)],
            lambda slot: vx.at[p, pl.ds(slot * rows, rows), col(h)],
            v_send.at[p], v_recv.at[p, h],
        )

    to_later(labs.at[2], lambda slot: labs.at[slot], lab_send, lab_recv)
    send_value(1, av_ref, 0)
    for p, v_ref in ((1, av_ref), (0, bv_ref)):
        vx[p, back:span, :] = v_ref[...]
    pltpu.make_async_copy(labs.at[pl.ds(0, 2)], labs.at[pl.ds(0, 2)], lab_recv).wait()

    lab_row = jnp.concatenate([labs[0, :1, :], labs[1, :1, :], labs[2, :1, :]], axis=1).astype(F32)
    place = lax.broadcasted_iota(jnp.int32, (1, span), 1)
    lab_row = jnp.where(place + (s - 2) * rows >= 0, lab_row, -1.0)
    own = lab_row[:, back:]
    r_id = lax.broadcasted_iota(jnp.int32, (rows, rows), 0)
    c_id = lax.broadcasted_iota(jnp.int32, (rows, rows), 1)
    lab_col = jnp.sum(jnp.where(r_id == c_id, own, 0.0), axis=1, keepdims=True)
    begin = jnp.sum(jnp.where(lab_row < lab_col, 1.0, 0.0), axis=1, keepdims=True)
    r_place = lax.broadcasted_iota(jnp.int32, (rows, 1), 0) + back
    positions = r_place.astype(F32) - begin
    angles = positions * rate_ref[:1, :]
    lane = lax.broadcasted_iota(jnp.int32, (rows, D), 1)
    cs[...] = jnp.cos(angles)
    sine = jnp.sin(angles)
    sn[...] = jnp.where(lane < D // 2, -sine, sine)
    wide = lax.broadcasted_iota(jnp.int32, (rows, span), 1)
    row_of = lax.broadcasted_iota(jnp.int32, (rows, span), 0) + back
    allowed = jnp.where(wide <= row_of, jnp.where(lab_row == lab_col, 0.0, -1e30), -1e30)
    bias[...] = allowed

    def turn(x, r0, n):
        x = x.astype(F32)
        y = x * cs[pl.ds(r0, n), :] + pltpu.roll(x, D // 2, 1) * sn[pl.ds(r0, n), :]
        return y.astype(BF16)

    for h in range(KEY_VALUE_HEADS):
        kx[1, back:span, h * D:(h + 1) * D] = turn(ak_ref[:, h * D:(h + 1) * D], 0, rows)
        send_key(1, h)
        if h + 1 < KEY_VALUE_HEADS:
            send_value(1, av_ref, h + 1)
    for h in range(KEY_VALUE_HEADS):
        kx[0, back:span, h * D:(h + 1) * D] = turn(bk_ref[:, h * D:(h + 1) * D], 0, rows)
        send_key(0, h)
        send_value(0, bv_ref, h)

    def arrived(p, h):
        there = kx.at[p, pl.ds(0, back), col(h)]
        pltpu.make_async_copy(there, there, k_recv.at[p, h]).wait()
        there = vx.at[p, pl.ds(0, back), col(h)]
        pltpu.make_async_copy(there, there, v_recv.at[p, h]).wait()

    factor = math.log2(math.e) / math.sqrt(D)
    keys = back + tile
    ones = jnp.ones((keys, D), BF16)

    def attend(p, q_ref, h, head, t):
        q = turn(q_ref[t * tile:(t + 1) * tile, col(head)], t * tile, tile)
        k = kx[p, t * tile:t * tile + keys, col(h)]
        v = vx[p, t * tile:t * tile + keys, col(h)]
        x = lax.dot_general(q, k, (((1,), (1,)), ((), ())), preferred_element_type=F32)
        x = x * factor + bias[t * tile:(t + 1) * tile, t * tile:t * tile + keys]
        e = jnp.exp2(x - jnp.max(x, axis=1, keepdims=True)).astype(BF16)
        o = jnp.dot(e, jnp.concatenate([v, ones], axis=1), preferred_element_type=F32)
        return (o[:, :D] / o[:, D:]).astype(BF16)

    def actor_group(h, c):
        arrived(1, h)

        def one_head(i, c):
            j = lax.rem(me // splits + 1 + i, GROUP)
            for t in range(rows // tile):
                att[h, j, t * tile:(t + 1) * tile, :] = attend(1, aq_ref, h, h * GROUP + j, t)
            for r in range(splits):
                to = j * splits + r
                src = att.at[h, j, pl.ds(r * part, part), :]

                @pl.when(to != me)
                def _():
                    pltpu.make_async_remote_copy(
                        src_ref=src, dst_ref=land.at[h, me],
                        send_sem=one_send.at[h], recv_sem=one_recv.at[h],
                        device_id={"dp": to}, device_id_type=MESH,
                    ).start()

                @pl.when(to == me)
                def _():
                    pltpu.make_async_copy(src, land.at[h, me], one_recv.at[h]).start()
            return c

        return lax.fori_loop(0, GROUP, one_head, c)

    lax.fori_loop(0, KEY_VALUE_HEADS, actor_group, 0)

    my_rows = pl.ds(pl.multiple_of(lax.rem(me, splits) * part, part), part)

    def base_group(h, c):
        arrived(0, h)

        def one_head(i, c):
            head = h * GROUP + i
            for t in range(rows // tile):
                bo[t * tile:(t + 1) * tile, col(head)] = attend(0, bq_ref, h, head, t)
            return c

        lax.fori_loop(0, GROUP, one_head, c)
        wide_col = pl.ds(pl.multiple_of(h * GROUP * D, GROUP * D), GROUP * D)
        pltpu.make_async_copy(bo.at[:, wide_col], base_out.at[:, wide_col], bo_sem).start()

        pltpu.make_async_copy(land.at[h], land.at[h], one_recv.at[h]).wait()

        def one_group(i, c):
            g = lax.rem(me + 1 + i, owners)

            def pick(u, val):
                return jnp.where(plan_ref[u] == g, land[h, u], val)

            fwd[h, g] = lax.fori_loop(1, owners, pick, land[h, 0], unroll=owners <= 8)
            dst = actor_out.at[my_rows, col(h * GROUP + me // splits)]

            @pl.when(g != me)
            def _():
                pltpu.make_async_remote_copy(
                    src_ref=fwd.at[h, g], dst_ref=dst,
                    send_sem=two_send.at[h], recv_sem=two_recv,
                    device_id={"dp": g}, device_id_type=MESH,
                ).start()

            @pl.when(g == me)
            def _():
                pltpu.make_async_copy(fwd.at[h, g], dst, two_recv).start()
            return c

        return lax.fori_loop(0, owners, one_group, c)

    lax.fori_loop(0, KEY_VALUE_HEADS, base_group, 0)

    def drain(ref, sem):
        pltpu.make_async_copy(ref, ref, sem).wait()

    drain(labs.at[pl.ds(0, 2)], lab_send)
    for p in range(2):
        drain(kx.at[p, pl.ds(0, back), :], k_send.at[p])
        drain(vx.at[p, pl.ds(0, back), :], v_send.at[p])
    for h in range(KEY_VALUE_HEADS):
        drain(land.at[h, pl.ds(0, owners - 1)], one_send.at[h])
    drain(base_out, bo_sem)
    for h in range(KEY_VALUE_HEADS):
        drain(land.at[h, pl.ds(0, owners - 1)], two_send.at[h])
    drain(actor_out, two_recv)


def per_device(owners, members, bq, bk, bv, aq, ak, av, labels, plan):
    rows = bq.shape[1]
    width = bq.shape[2]
    narrow = bk.shape[2]
    D = HEAD_SIZE
    part = rows // (owners // GROUP)
    half = np.arange(D) % (D // 2)
    rates = np.exp(half.astype(np.float64) * (-2.0 * math.log(THETA) / D)).astype(np.float32)
    rates = jnp.asarray(np.broadcast_to(rates, (8, D)))
    vmem = pl.BlockSpec(memory_space=pltpu.VMEM)
    out = jax.ShapeDtypeStruct((rows, width), BF16)
    dma = pltpu.SemaphoreType.DMA
    KV = KEY_VALUE_HEADS
    call = pl.pallas_call(
        functools.partial(kernel, owners, members, rows, rows // 2),
        out_shape=(out, out),
        in_specs=[pl.BlockSpec(memory_space=pltpu.SMEM)] + [vmem] * 8,
        out_specs=(pl.BlockSpec(memory_space=pl.ANY), pl.BlockSpec(memory_space=pl.ANY)),
        scratch_shapes=[
            pltpu.VMEM((3, 8, rows), jnp.int32),
            pltpu.VMEM((rows, D), F32),
            pltpu.VMEM((rows, D), F32),
            pltpu.VMEM((rows, 3 * rows), F32),
            pltpu.VMEM((2, 3 * rows, narrow), BF16),
            pltpu.VMEM((2, 3 * rows, narrow), BF16),
            pltpu.VMEM((KV, GROUP, rows, D), BF16),
            pltpu.VMEM((KV, owners, part, D), BF16),
            pltpu.VMEM((KV, owners, part, D), BF16),
            pltpu.VMEM((rows, width), BF16),
            dma, dma, dma((2,)), dma((2,)), dma((2, KV)), dma((2, KV)),
            dma((KV,)), dma((KV,)), dma((KV,)), dma, dma,
        ],
        compiler_params=pltpu.CompilerParams(
            collective_id=0, has_side_effects=True, vmem_limit_bytes=48 * 1024 * 1024
        ),
        cost_estimate=pl.CostEstimate(
            flops=2 * 4 * rows * (5 * rows // 2) * width, bytes_accessed=8 * rows * width,
            transcendentals=0,
        ),
    )
    base, actor = call(plan, labels, rates, bq[0], bk[0], bv[0], aq[0], ak[0], av[0])
    return base[None], actor[None]


def solution(mesh):
    rows3 = P("dp", "sp", None)
    return jax.shard_map(
        functools.partial(per_device, mesh.shape["dp"], mesh.shape["sp"]),
        mesh=mesh,
        in_specs=(rows3,) * 6 + (P("dp", "sp"), P()),
        out_specs=(rows3, rows3),
        check_vma=False,
    )
```

```python
import functools
import math

import jax
import jax.numpy as jnp
import numpy as np
from jax import lax
from jax.experimental import pallas as pl
from jax.experimental.pallas import tpu as pltpu
from jax.sharding import PartitionSpec as P

QUERY_HEADS = 32
KEY_VALUE_HEADS = 4
HEAD_SIZE = 128
GROUP = QUERY_HEADS // KEY_VALUE_HEADS
THETA = 1000000.0
MESH = pl.DeviceIdType.MESH
BF16 = jnp.bfloat16
F32 = jnp.float32


def kernel(
    owners, members, rows, tile, cap,
    plan_ref, lab_ref, rate_ref, bq_hbm, bk_hbm, bv_hbm, aq_hbm, ak_hbm, av_hbm,
    base_out, actor_out,
    labs, cs, sn, bias, qs, ks, kx, vx, att, land, fwd, bo, out_box, in_box,
    q_sem, k_sem, v_sem,
    lab_send, lab_recv, k_send, v_send, k_recv, v_recv,
    one_send, one_recv, two_send, two_recv, bo_sem, box_send, box_recv,
):
    D = HEAD_SIZE
    me = lax.axis_index("dp")
    s = lax.axis_index("sp")
    back = 2 * rows
    span = 3 * rows
    splits = owners // GROUP
    part = rows // splits

    loads = {}
    for p, q_hbm, k_hbm, v_hbm in ((1, aq_hbm, ak_hbm, av_hbm), (0, bq_hbm, bk_hbm, bv_hbm)):
        loads[p] = (
            pltpu.make_async_copy(q_hbm, qs.at[p], q_sem.at[p]),
            pltpu.make_async_copy(k_hbm, ks.at[p], k_sem.at[p]),
            pltpu.make_async_copy(v_hbm, vx.at[p, pl.ds(back, rows), :], v_sem.at[p]),
        )
    for p in (1, 0):
        for load in (loads[p][2], loads[p][1], loads[p][0]):
            load.start()

    def col(h):
        return pl.ds(pl.multiple_of(h * D, D), D)

    labs[2] = jnp.broadcast_to(lab_ref[...], labs.shape[1:])
    barrier = pltpu.get_barrier_semaphore()

    def greet_owner(j, c):
        pl.semaphore_signal(
            barrier, inc=1, device_id={"dp": lax.rem(me + j, owners)}, device_id_type=MESH
        )
        return c

    lax.fori_loop(1, owners, greet_owner, 0)
    for j in range(1, members):
        pl.semaphore_signal(
            barrier, inc=1, device_id={"sp": lax.rem(s + j, members)}, device_id_type=MESH
        )
    pl.semaphore_wait(barrier, owners - 1 + members - 1)

    def to_later(src, dst_of, send_sem, recv_sem):
        for step in (1, 2):
            pltpu.make_async_remote_copy(
                src_ref=src,
                dst_ref=dst_of(2 - step),
                send_sem=send_sem,
                recv_sem=recv_sem,
                device_id={"sp": lax.rem(s + step, members)},
                device_id_type=MESH,
            ).start()

    def send_key(p, h):
        to_later(
            kx.at[p, pl.ds(back, rows), col(h)],
            lambda slot: kx.at[p, pl.ds(slot * rows, rows), col(h)],
            k_send.at[p], k_recv.at[p, h],
        )

    def send_value(p, h):
        to_later(
            vx.at[p, pl.ds(back, rows), col(h)],
            lambda slot: vx.at[p, pl.ds(slot * rows, rows), col(h)],
            v_send.at[p], v_recv.at[p, h],
        )

    to_later(labs.at[2], lambda slot: labs.at[slot], lab_send, lab_recv)
    loads[1][2].wait()
    send_value(1, 0)
    pltpu.make_async_copy(labs.at[pl.ds(0, 2)], labs.at[pl.ds(0, 2)], lab_recv).wait()

    lab_row = jnp.concatenate([labs[0, :1, :], labs[1, :1, :], labs[2, :1, :]], axis=1).astype(F32)
    place = lax.broadcasted_iota(jnp.int32, (1, span), 1)
    lab_row = jnp.where(place + (s - 2) * rows >= 0, lab_row, -1.0)
    own = lab_row[:, back:]
    r_id = lax.broadcasted_iota(jnp.int32, (rows, rows), 0)
    c_id = lax.broadcasted_iota(jnp.int32, (rows, rows), 1)
    lab_col = jnp.sum(jnp.where(r_id == c_id, own, 0.0), axis=1, keepdims=True)
    begin = jnp.sum(jnp.where(lab_row < lab_col, 1.0, 0.0), axis=1, keepdims=True)
    r_place = lax.broadcasted_iota(jnp.int32, (rows, 1), 0) + back
    positions = r_place.astype(F32) - begin
    angles = positions * rate_ref[:1, :]
    lane = lax.broadcasted_iota(jnp.int32, (rows, D), 1)
    cs[...] = jnp.cos(angles)
    sine = jnp.sin(angles)
    sn[...] = jnp.where(lane < D // 2, -sine, sine)
    wide = lax.broadcasted_iota(jnp.int32, (rows, span), 1)
    row_of = lax.broadcasted_iota(jnp.int32, (rows, span), 0) + back
    allowed = jnp.where(wide <= row_of, jnp.where(lab_row == lab_col, 0.0, -1e30), -1e30)
    bias[...] = allowed

    def turn(x, r0, n):
        x = x.astype(F32)
        y = x * cs[pl.ds(r0, n), :] + pltpu.roll(x, D // 2, 1) * sn[pl.ds(r0, n), :]
        return y.astype(BF16)

    loads[1][1].wait()
    for h in range(KEY_VALUE_HEADS):
        kx[1, back:span, h * D:(h + 1) * D] = turn(ks[1, :, h * D:(h + 1) * D], 0, rows)
        send_key(1, h)
        if h + 1 < KEY_VALUE_HEADS:
            send_value(1, h + 1)
    loads[0][2].wait()
    loads[0][1].wait()
    for h in range(KEY_VALUE_HEADS):
        kx[0, back:span, h * D:(h + 1) * D] = turn(ks[0, :, h * D:(h + 1) * D], 0, rows)
        send_key(0, h)
        send_value(0, h)
    loads[1][0].wait()
    loads[0][0].wait()

    def arrived(p, h):
        there = kx.at[p, pl.ds(0, back), col(h)]
        pltpu.make_async_copy(there, there, k_recv.at[p, h]).wait()
        there = vx.at[p, pl.ds(0, back), col(h)]
        pltpu.make_async_copy(there, there, v_recv.at[p, h]).wait()

    factor = math.log2(math.e) / math.sqrt(D)
    keys = back + tile
    ones = jnp.ones((keys, D), BF16)

    def attend(p, h, head, t):
        q = turn(qs[p, t * tile:(t + 1) * tile, col(head)], t * tile, tile)
        k = kx[p, t * tile:t * tile + keys, col(h)]
        v = vx[p, t * tile:t * tile + keys, col(h)]
        x = lax.dot_general(q, k, (((1,), (1,)), ((), ())), preferred_element_type=F32)
        x = x * factor + bias[t * tile:(t + 1) * tile, t * tile:t * tile + keys]
        e = jnp.exp2(x - jnp.max(x, axis=1, keepdims=True)).astype(BF16)
        o = jnp.dot(e, jnp.concatenate([v, ones], axis=1), preferred_element_type=F32)
        return (o[:, :D] / o[:, D:]).astype(BF16)

    def move(src, dst, owner, send_sem, recv_sem):
        @pl.when(owner != me)
        def _():
            pltpu.make_async_remote_copy(
                src_ref=src, dst_ref=dst, send_sem=send_sem, recv_sem=recv_sem,
                device_id={"dp": owner}, device_id_type=MESH,
            ).start()

        @pl.when(owner == me)
        def _():
            pltpu.make_async_copy(src, dst, recv_sem).start()

    def drain(ref, sem):
        pltpu.make_async_copy(ref, ref, sem).wait()

    def base_group(h):
        arrived(0, h)

        def two_heads(i, c):
            for k in range(2):
                head = h * GROUP + 2 * i + k
                for t in range(rows // tile):
                    bo[t * tile:(t + 1) * tile, col(head)] = attend(0, h, head, t)
            return c

        lax.fori_loop(0, GROUP // 2, two_heads, 0)
        wide_col = pl.ds(pl.multiple_of(h * GROUP * D, GROUP * D), GROUP * D)
        pltpu.make_async_copy(bo.at[:, wide_col], base_out.at[:, wide_col], bo_sem).start()

    if cap is None:
        def actor_group(h, c):
            arrived(1, h)

            def one_head(i, c):
                j = lax.rem(me // splits + 1 + i, GROUP)
                for t in range(rows // tile):
                    att[h, j, t * tile:(t + 1) * tile, :] = attend(1, h, h * GROUP + j, t)
                for r in range(splits):
                    move(
                        att.at[h, j, pl.ds(r * part, part), :], land.at[h, me], j * splits + r,
                        one_send.at[h], one_recv.at[h],
                    )
                return c

            return lax.fori_loop(0, GROUP, one_head, c)

        my_rows = pl.ds(pl.multiple_of(lax.rem(me, splits) * part, part), part)

        def second_group(h, c):
            base_group(h)
            drain(land.at[h], one_recv.at[h])

            def one_group(i, c):
                g = lax.rem(me + 1 + i, owners)

                def pick(u, val):
                    return jnp.where(plan_ref[u] == g, land[h, u], val)

                fwd[h, g] = lax.fori_loop(1, owners, pick, land[h, 0], unroll=owners <= 8)
                move(
                    fwd.at[h, g], actor_out.at[my_rows, col(h * GROUP + me // splits)], g,
                    two_send.at[h], two_recv,
                )
                return c

            return lax.fori_loop(0, owners, one_group, c)

        moved = owners - 1
    else:
        half = owners // 2
        per = GROUP // half
        place_of = lax.rem(me, half)
        mine = me - place_of
        other = lax.rem(mine + half, owners)

        def ranks(first):
            taken, groups, out = 0, [], []
            for p in range(half):
                g = plan_ref[first + p]
                near = jnp.where(g >= first, 1, 0) * jnp.where(g < first + half, 1, 0)
                groups.append(g)
                out.append(jnp.where(near == 1, -1, taken))
                taken = taken + 1 - near
            return groups, out

        my_groups, my_ranks = ranks(mine)
        far_groups, far_ranks = ranks(other)

        def actor_piece(h, c):
            arrived(1, h)

            def one_piece(i, c):
                j = lax.rem(place_of + 1 + i, half)
                for k in range(per):
                    for t in range(rows // tile):
                        att[h, j, t * tile:(t + 1) * tile, k * D:(k + 1) * D] = attend(
                            1, h, h * GROUP + j * per + k, t
                        )
                move(att.at[h, j], land.at[h, place_of], mine + j, one_send.at[h], one_recv.at[h])
                return c

            lax.fori_loop(0, half, one_piece, 0)

            @pl.when(h >= 1)
            def _():
                cross(h - 1)

            return c

        def cross(h):
            drain(land.at[h], one_recv.at[h])
            for slot in range(cap):
                val = land[h, 0]
                for p in range(1, half):
                    val = jnp.where(my_ranks[p] == slot, land[h, p], val)
                out_box[h, slot] = val
            pltpu.make_async_remote_copy(
                src_ref=out_box.at[h], dst_ref=in_box.at[h],
                send_sem=box_send.at[h], recv_sem=box_recv.at[h],
                device_id={"dp": lax.rem(me + half, owners)}, device_id_type=MESH,
            ).start()

        wide = per * D
        actor_group = actor_piece

        def second_group(h, c):
            base_group(h)

            @pl.when(h == 0)
            def _():
                cross(KEY_VALUE_HEADS - 1)

            drain(in_box.at[h], box_recv.at[h])

            def one_group(i, c):
                r = lax.rem(place_of + 1 + i, half)
                g = mine + r
                val = land[h, 0]
                for p in range(1, half):
                    val = jnp.where(my_groups[p] == g, land[h, p], val)
                for slot in range(cap):
                    hit = 0
                    for p in range(half):
                        hit = hit + jnp.where(far_groups[p] == g, 1, 0) * jnp.where(
                            far_ranks[p] == slot, 1, 0
                        )
                    val = jnp.where(hit == 1, in_box[h, slot], val)
                fwd[h, r] = val
                there = pl.ds(pl.multiple_of((h * half + place_of) * wide, wide), wide)
                move(fwd.at[h, r], actor_out.at[:, there], g, two_send.at[h], two_recv)
                return c

            return lax.fori_loop(0, half, one_group, c)

        moved = half - 1

    lax.fori_loop(0, KEY_VALUE_HEADS, actor_group, 0)
    lax.fori_loop(0, KEY_VALUE_HEADS, second_group, 0)

    drain(labs.at[pl.ds(0, 2)], lab_send)
    for p in range(2):
        drain(kx.at[p, pl.ds(0, back), :], k_send.at[p])
        drain(vx.at[p, pl.ds(0, back), :], v_send.at[p])
    for h in range(KEY_VALUE_HEADS):
        drain(land.at[h, pl.ds(0, moved)], one_send.at[h])
    drain(base_out, bo_sem)
    for h in range(KEY_VALUE_HEADS):
        drain(land.at[h, pl.ds(0, moved)], two_send.at[h])
        if cap is not None:
            drain(out_box.at[h], box_send.at[h])
    drain(actor_out, two_recv)


def per_device(owners, members, bq, bk, bv, aq, ak, av, labels, plan):
    rows = bq.shape[1]
    width = bq.shape[2]
    narrow = bk.shape[2]
    D = HEAD_SIZE
    half = np.arange(D) % (D // 2)
    rates = np.exp(half.astype(np.float64) * (-2.0 * math.log(THETA) / D)).astype(np.float32)
    rates = jnp.asarray(np.broadcast_to(rates, (8, D)))
    vmem = pl.BlockSpec(memory_space=pltpu.VMEM)
    hbm = pl.BlockSpec(memory_space=pl.ANY)
    out = jax.ShapeDtypeStruct((rows, width), BF16)
    dma = pltpu.SemaphoreType.DMA
    KV = KEY_VALUE_HEADS

    def call(cap, number, *args):
        if cap is None:
            part = (owners, rows // (owners // GROUP), D)
            made = (GROUP, rows, D)
            box = (1, 1, 16, D)
        else:
            part = made = (owners // 2, rows, GROUP // (owners // 2) * D)
            box = (KV, cap) + part[1:]
        return pl.pallas_call(
            functools.partial(kernel, owners, members, rows, rows // 2, cap),
            out_shape=(out, out),
            in_specs=[pl.BlockSpec(memory_space=pltpu.SMEM)] + [vmem] * 2 + [hbm] * 6,
            out_specs=(hbm, hbm),
            scratch_shapes=[
                pltpu.VMEM((3, 8, rows), jnp.int32),
                pltpu.VMEM((rows, D), F32),
                pltpu.VMEM((rows, D), F32),
                pltpu.VMEM((rows, 3 * rows), F32),
                pltpu.VMEM((2, rows, width), BF16),
                pltpu.VMEM((2, rows, narrow), BF16),
                pltpu.VMEM((2, 3 * rows, narrow), BF16),
                pltpu.VMEM((2, 3 * rows, narrow), BF16),
                pltpu.VMEM((KV,) + made, BF16),
                pltpu.VMEM((KV,) + part, BF16),
                pltpu.VMEM((KV,) + part, BF16),
                pltpu.VMEM((rows, width), BF16),
                pltpu.VMEM(box, BF16),
                pltpu.VMEM(box, BF16),
                dma((2,)), dma((2,)), dma((2,)),
                dma, dma, dma((2,)), dma((2,)), dma((2, KV)), dma((2, KV)),
                dma((KV,)), dma((KV,)), dma((KV,)), dma, dma, dma((KV,)), dma((KV,)),
            ],
            compiler_params=pltpu.CompilerParams(
                collective_id=number, has_side_effects=True, vmem_limit_bytes=60 * 1024 * 1024
            ),
            cost_estimate=pl.CostEstimate(
                flops=2 * 4 * rows * (5 * rows // 2) * width, bytes_accessed=8 * rows * width,
                transcendentals=0,
            ),
        )(*args)

    args = (plan, labels, rates, bq[0], bk[0], bv[0], aq[0], ak[0], av[0])
    if owners != 8:
        base, actor = call(None, 0, *args)
    else:
        leaving = jnp.sum((plan[: owners // 2] >= owners // 2).astype(jnp.int32))
        caps = range(1, owners // 2 + 1)
        base, actor = lax.switch(
            jnp.maximum(leaving, 1) - 1,
            [functools.partial(call, cap, cap) for cap in caps],
            *args,
        )
    return base[None], actor[None]


def solution(mesh):
    rows3 = P("dp", "sp", None)
    return jax.shard_map(
        functools.partial(per_device, mesh.shape["dp"], mesh.shape["sp"]),
        mesh=mesh,
        in_specs=(rows3,) * 6 + (P("dp", "sp"), P()),
        out_specs=(rows3, rows3),
        check_vma=False,
    )
```

```python
import functools
import math

import jax
import jax.numpy as jnp
import numpy as np
from jax import lax
from jax.experimental import pallas as pl
from jax.experimental.pallas import tpu as pltpu
from jax.sharding import PartitionSpec as P

QUERY_HEADS = 32
KEY_VALUE_HEADS = 4
HEAD_SIZE = 128
GROUP = QUERY_HEADS // KEY_VALUE_HEADS
INNER, OUTER = 3, 1
THETA = 1000000.0
MESH = pl.DeviceIdType.MESH
BF16 = jnp.bfloat16
F32 = jnp.float32


def kernel(
    owners, members, rows, tile, cap,
    plan_ref, lab_ref, rate_ref, bq_hbm, bk_hbm, bv_hbm, aq_hbm, ak_hbm, av_hbm,
    base_out, actor_out,
    labs, cs, sn, bias, qs, ks, kx, vx, att, land, fwd, bo, out_box, in_box,
    q_sem, k_sem, v_sem,
    lab_send, lab_recv, k_send, v_send, k_recv, v_recv,
    one_send, one_recv, two_send, two_recv, bo_sem, box_send, box_recv,
):
    D = HEAD_SIZE
    me = lax.axis_index("dp")
    s = lax.axis_index("sp")
    back = 2 * rows
    span = 3 * rows
    splits = owners // GROUP
    part = rows // splits

    loads = {}
    for p, q_hbm, k_hbm, v_hbm in ((1, aq_hbm, ak_hbm, av_hbm), (0, bq_hbm, bk_hbm, bv_hbm)):
        loads[p] = (
            pltpu.make_async_copy(q_hbm, qs.at[p], q_sem.at[p]),
            pltpu.make_async_copy(k_hbm, ks.at[p], k_sem.at[p]),
            pltpu.make_async_copy(v_hbm, vx.at[p, pl.ds(back, rows), :], v_sem.at[p]),
        )
    for p in (1, 0):
        for load in (loads[p][2], loads[p][1], loads[p][0]):
            load.start()

    def col(h):
        return pl.ds(pl.multiple_of(h * D, D), D)

    labs[2] = jnp.broadcast_to(lab_ref[...], labs.shape[1:])
    barrier = pltpu.get_barrier_semaphore()

    def greet_owner(j, c):
        pl.semaphore_signal(
            barrier, inc=1, device_id={"dp": lax.rem(me + j, owners)}, device_id_type=MESH
        )
        return c

    lax.fori_loop(1, owners, greet_owner, 0)
    for j in range(1, members):
        pl.semaphore_signal(
            barrier, inc=1, device_id={"sp": lax.rem(s + j, members)}, device_id_type=MESH
        )
    pl.semaphore_wait(barrier, owners - 1 + members - 1)

    def to_later(src, dst_of, send_sem, recv_sem):
        for step in (1, 2):
            pltpu.make_async_remote_copy(
                src_ref=src,
                dst_ref=dst_of(2 - step),
                send_sem=send_sem,
                recv_sem=recv_sem,
                device_id={"sp": lax.rem(s + step, members)},
                device_id_type=MESH,
            ).start()

    def send_key(p, h):
        to_later(
            kx.at[p, pl.ds(back, rows), col(h)],
            lambda slot: kx.at[p, pl.ds(slot * rows, rows), col(h)],
            k_send.at[p], k_recv.at[p, h],
        )

    def send_value(p, h):
        to_later(
            vx.at[p, pl.ds(back, rows), col(h)],
            lambda slot: vx.at[p, pl.ds(slot * rows, rows), col(h)],
            v_send.at[p], v_recv.at[p, h],
        )

    to_later(labs.at[2], lambda slot: labs.at[slot], lab_send, lab_recv)
    loads[1][2].wait()
    send_value(1, 0)
    pltpu.make_async_copy(labs.at[pl.ds(0, 2)], labs.at[pl.ds(0, 2)], lab_recv).wait()

    lab_row = jnp.concatenate([labs[0, :1, :], labs[1, :1, :], labs[2, :1, :]], axis=1).astype(F32)
    place = lax.broadcasted_iota(jnp.int32, (1, span), 1)
    lab_row = jnp.where(place + (s - 2) * rows >= 0, lab_row, -1.0)
    own = lab_row[:, back:]
    r_id = lax.broadcasted_iota(jnp.int32, (rows, rows), 0)
    c_id = lax.broadcasted_iota(jnp.int32, (rows, rows), 1)
    lab_col = jnp.sum(jnp.where(r_id == c_id, own, 0.0), axis=1, keepdims=True)
    begin = jnp.sum(jnp.where(lab_row < lab_col, 1.0, 0.0), axis=1, keepdims=True)
    r_place = lax.broadcasted_iota(jnp.int32, (rows, 1), 0) + back
    positions = r_place.astype(F32) - begin
    angles = positions * rate_ref[...]
    lane = lax.broadcasted_iota(jnp.int32, (rows, D), 1)
    cs[...] = jnp.cos(angles)
    sine = jnp.sin(angles)
    sn[...] = jnp.where(lane < D // 2, -sine, sine)
    wide = lax.broadcasted_iota(jnp.int32, (rows, span), 1)
    row_of = lax.broadcasted_iota(jnp.int32, (rows, span), 0) + back
    allowed = jnp.where(wide <= row_of, jnp.where(lab_row == lab_col, 0.0, -1e30), -1e30)
    bias[...] = allowed

    def turn(x, r0, n):
        x = x.astype(F32)
        y = x * cs[pl.ds(r0, n), :] + pltpu.roll(x, D // 2, 1) * sn[pl.ds(r0, n), :]
        return y.astype(BF16)

    loads[1][1].wait()
    for h in range(KEY_VALUE_HEADS):
        kx[1, back:span, h * D:(h + 1) * D] = turn(ks[1, :, h * D:(h + 1) * D], 0, rows)
        send_key(1, h)
        if h + 1 < KEY_VALUE_HEADS:
            send_value(1, h + 1)
    loads[0][2].wait()
    loads[0][1].wait()
    for h in range(KEY_VALUE_HEADS):
        kx[0, back:span, h * D:(h + 1) * D] = turn(ks[0, :, h * D:(h + 1) * D], 0, rows)
        send_key(0, h)
        send_value(0, h)
    loads[1][0].wait()
    loads[0][0].wait()

    def arrived(p, h):
        there = kx.at[p, pl.ds(0, back), col(h)]
        pltpu.make_async_copy(there, there, k_recv.at[p, h]).wait()
        there = vx.at[p, pl.ds(0, back), col(h)]
        pltpu.make_async_copy(there, there, v_recv.at[p, h]).wait()

    factor = math.log2(math.e) / math.sqrt(D)
    keys = back + tile
    ones = jnp.ones((keys, D), BF16)

    def attend(p, h, head, t):
        q = turn(qs[p, t * tile:(t + 1) * tile, col(head)], t * tile, tile)
        k = kx[p, t * tile:t * tile + keys, col(h)]
        v = vx[p, t * tile:t * tile + keys, col(h)]
        x = lax.dot_general(q, k, (((1,), (1,)), ((), ())), preferred_element_type=F32)
        x = x * factor + bias[t * tile:(t + 1) * tile, t * tile:t * tile + keys]
        e = jnp.exp2(x - jnp.max(x, axis=1, keepdims=True)).astype(BF16)
        o = jnp.dot(e, jnp.concatenate([v, ones], axis=1), preferred_element_type=F32)
        return (o[:, :D] / o[:, D:]).astype(BF16)

    def move(src, dst, owner, send_sem, recv_sem):
        @pl.when(owner != me)
        def _():
            pltpu.make_async_remote_copy(
                src_ref=src, dst_ref=dst, send_sem=send_sem, recv_sem=recv_sem,
                device_id={"dp": owner}, device_id_type=MESH,
            ).start()

        @pl.when(owner == me)
        def _():
            pltpu.make_async_copy(src, dst, recv_sem).start()

    def drain(ref, sem):
        pltpu.make_async_copy(ref, ref, sem).wait()

    def base_group(h):
        arrived(0, h)

        def two_heads(i, c):
            for k in range(2):
                head = h * GROUP + 2 * i + k
                for t in range(rows // tile):
                    bo[t * tile:(t + 1) * tile, col(head)] = attend(0, h, head, t)
            return c

        lax.fori_loop(0, GROUP // 2, two_heads, 0)
        wide_col = pl.ds(pl.multiple_of(h * GROUP * D, GROUP * D), GROUP * D)
        pltpu.make_async_copy(bo.at[:, wide_col], base_out.at[:, wide_col], bo_sem).start()

    if cap is None:
        def actor_group(h, c):
            arrived(1, h)

            def one_head(i, c):
                j = lax.rem(me // splits + 1 + i, GROUP)
                for t in range(rows // tile):
                    att[h, j, t * tile:(t + 1) * tile, :] = attend(1, h, h * GROUP + j, t)
                for r in range(splits):
                    move(
                        att.at[h, j, pl.ds(r * part, part), :], land.at[h, me], j * splits + r,
                        one_send.at[h], one_recv.at[h],
                    )
                return c

            return lax.fori_loop(0, GROUP, one_head, c)

        my_rows = pl.ds(pl.multiple_of(lax.rem(me, splits) * part, part), part)

        def second_group(h, c):
            base_group(h)
            drain(land.at[h], one_recv.at[h])

            def one_group(i, c):
                g = lax.rem(me + 1 + i, owners)

                def pick(u, val):
                    return jnp.where(plan_ref[u] == g, land[h, u], val)

                fwd[h, g] = lax.fori_loop(1, owners, pick, land[h, 0], unroll=owners <= 8)
                move(
                    fwd.at[h, g], actor_out.at[my_rows, col(h * GROUP + me // splits)], g,
                    two_send.at[h], two_recv,
                )
                return c

            return lax.fori_loop(0, owners, one_group, c)

    else:
        half = owners // 2
        pair = half // 2
        upper = me // half
        mine = upper * half
        other = half - mine
        place = me - mine
        side = lax.rem(place, pair)
        depth = jnp.where(upper == 0, place // pair, 1 - place // pair)
        mirror = other + jnp.where(upper == 0, 1 - depth, depth) * pair + side
        count = jnp.where(depth == 1, INNER, OUTER)
        first = jnp.where(depth == 1, pair * OUTER + side * INNER, side * OUTER)

        def ranks(start):
            taken, groups, out = 0, [], []
            for p in range(half):
                g = plan_ref[start + p]
                near = jnp.where(g >= start, 1, 0) * jnp.where(g < start + half, 1, 0)
                groups.append(g)
                out.append(jnp.where(near == 1, -1, taken))
                taken = taken + 1 - near
            return groups, out

        my_groups, my_ranks = ranks(mine)
        far_groups, far_ranks = ranks(other)

        def actor_piece(h, c):
            arrived(1, h)

            def two_heads(i, c):
                j = lax.rem(2 * place + 2 * i, GROUP)
                for k in range(2):
                    for t in range(rows // tile):
                        att[h, j + k, t * tile:(t + 1) * tile, :] = attend(
                            1, h, h * GROUP + j + k, t
                        )
                for k in range(2):
                    deep = jnp.where(j + k >= pair * OUTER, 1, 0)
                    rest = j + k - deep * pair * OUTER
                    share = jnp.where(deep == 1, INNER, OUTER)
                    line = jnp.where(upper == 0, deep, 1 - deep)
                    turn_of = jnp.where(rest >= share, 1, 0)
                    unit = rest - turn_of * share
                    move(
                        att.at[h, j + k], land.at[h, unit, place],
                        mine + line * pair + turn_of,
                        one_send.at[h], one_recv.at[h, unit],
                    )
                return c

            lax.fori_loop(0, GROUP // 2, two_heads, 0)

            @pl.when(h >= 1)
            def _():
                cross(h - 1)

            return c

        def cross(h):
            def unit(k, c):
                drain(land.at[h, k], one_recv.at[h, k])
                for slot in range(cap):
                    val = land[h, k, 0]
                    for p in range(1, half):
                        val = jnp.where(my_ranks[p] == slot, land[h, k, p], val)
                    out_box[h, k, slot] = val
                pltpu.make_async_remote_copy(
                    src_ref=out_box.at[h, k], dst_ref=in_box.at[h, k],
                    send_sem=box_send.at[h, k], recv_sem=box_recv.at[h, k],
                    device_id={"dp": mirror}, device_id_type=MESH,
                ).start()
                return c

            lax.fori_loop(0, count, unit, 0)

        actor_group = actor_piece

        def second_group(h, c):
            base_group(h)

            @pl.when(h == 0)
            def _():
                cross(KEY_VALUE_HEADS - 1)

            def unit(k, c):
                drain(in_box.at[h, k], box_recv.at[h, k])

                def one_group(i, c):
                    r = lax.rem(place + 1 + i, half)
                    g = mine + r
                    val = land[h, k, 0]
                    for p in range(1, half):
                        val = jnp.where(my_groups[p] == g, land[h, k, p], val)
                    for slot in range(cap):
                        hit = 0
                        for p in range(half):
                            hit = hit + jnp.where(far_groups[p] == g, 1, 0) * jnp.where(
                                far_ranks[p] == slot, 1, 0
                            )
                        val = jnp.where(hit == 1, in_box[h, k, slot], val)
                    fwd[h, k, r] = val
                    move(
                        fwd.at[h, k, r], actor_out.at[:, col(h * GROUP + first + k)], g,
                        two_send.at[h, k], two_recv,
                    )
                    return c

                return lax.fori_loop(0, half, one_group, c)

            return lax.fori_loop(0, count, unit, c)

    lax.fori_loop(0, KEY_VALUE_HEADS, actor_group, 0)
    lax.fori_loop(0, KEY_VALUE_HEADS, second_group, 0)

    drain(labs.at[pl.ds(0, 2)], lab_send)
    for p in range(2):
        drain(kx.at[p, pl.ds(0, back), :], k_send.at[p])
        drain(vx.at[p, pl.ds(0, back), :], v_send.at[p])
    drain(base_out, bo_sem)
    for h in range(KEY_VALUE_HEADS):
        if cap is None:
            drain(land.at[h, pl.ds(0, owners - 1)], one_send.at[h])
            drain(land.at[h, pl.ds(0, owners - 1)], two_send.at[h])
        else:
            for kind, share in enumerate((OUTER, INNER)):
                @pl.when(depth == kind)
                def _():
                    drain(att.at[h, pl.ds(0, GROUP - share)], one_send.at[h])
                    for k in range(share):
                        drain(out_box.at[h, k], box_send.at[h, k])
                        drain(fwd.at[h, k, pl.ds(0, half - 1)], two_send.at[h, k])
    drain(actor_out, two_recv)


def per_device(owners, members, bq, bk, bv, aq, ak, av, labels, plan):
    rows = bq.shape[1]
    width = bq.shape[2]
    narrow = bk.shape[2]
    D = HEAD_SIZE
    half = np.arange(D) % (D // 2)
    rates = np.exp(half.astype(np.float64) * (-2.0 * math.log(THETA) / D)).astype(np.float32)
    rates = jnp.asarray(rates.reshape(1, D))
    vmem = pl.BlockSpec(memory_space=pltpu.VMEM)
    hbm = pl.BlockSpec(memory_space=pl.ANY)
    out = jax.ShapeDtypeStruct((rows, width), BF16)
    dma = pltpu.SemaphoreType.DMA
    KV = KEY_VALUE_HEADS

    def call(cap, number, *args):
        if cap is None:
            part = (owners, rows // (owners // GROUP), D)
            box = (1, 1, 16, D)
            sems = (KV,)
        else:
            part = (INNER, owners // 2, rows, D)
            box = (KV, INNER, cap, rows, D)
            sems = (KV, INNER)
        return pl.pallas_call(
            functools.partial(kernel, owners, members, rows, rows // 2, cap),
            out_shape=(out, out),
            in_specs=[pl.BlockSpec(memory_space=pltpu.SMEM)] + [vmem] * 2 + [hbm] * 6,
            out_specs=(hbm, hbm),
            scratch_shapes=[
                pltpu.VMEM((3, 8, rows), jnp.int32),
                pltpu.VMEM((rows, D), F32),
                pltpu.VMEM((rows, D), F32),
                pltpu.VMEM((rows, 3 * rows), F32),
                pltpu.VMEM((2, rows, width), BF16),
                pltpu.VMEM((2, rows, narrow), BF16),
                pltpu.VMEM((2, 3 * rows, narrow), BF16),
                pltpu.VMEM((2, 3 * rows, narrow), BF16),
                pltpu.VMEM((KV, GROUP, rows, D), BF16),
                pltpu.VMEM((KV,) + part, BF16),
                pltpu.VMEM((KV,) + part, BF16),
                pltpu.VMEM((rows, width), BF16),
                pltpu.VMEM(box, BF16),
                pltpu.VMEM(box, BF16),
                dma((2,)), dma((2,)), dma((2,)),
                dma, dma, dma((2,)), dma((2,)), dma((2, KV)), dma((2, KV)),
                dma((KV,)), dma(sems), dma(sems), dma, dma, dma(sems), dma(sems),
            ],
            compiler_params=pltpu.CompilerParams(
                collective_id=number, has_side_effects=True, vmem_limit_bytes=60 * 1024 * 1024
            ),
            cost_estimate=pl.CostEstimate(
                flops=2 * 4 * rows * (5 * rows // 2) * width, bytes_accessed=8 * rows * width,
                transcendentals=0,
            ),
        )(*args)

    args = (plan, labels, rates, bq[0], bk[0], bv[0], aq[0], ak[0], av[0])
    if owners != 8:
        base, actor = call(None, 0, *args)
    else:
        leaving = jnp.sum((plan[: owners // 2] >= owners // 2).astype(jnp.int32))
        caps = range(1, owners // 2 + 1)
        base, actor = lax.switch(
            jnp.maximum(leaving, 1) - 1,
            [functools.partial(call, cap, cap) for cap in caps],
            *args,
        )
    return base[None], actor[None]


def solution(mesh):
    rows3 = P("dp", "sp", None)
    return jax.shard_map(
        functools.partial(per_device, mesh.shape["dp"], mesh.shape["sp"]),
        mesh=mesh,
        in_specs=(rows3,) * 6 + (P("dp", "sp"), P()),
        out_specs=(rows3, rows3),
        check_vma=False,
    )
```

```python
import functools
import math

import jax
import jax.numpy as jnp
import numpy as np
from jax import lax
from jax.experimental import pallas as pl
from jax.experimental.pallas import tpu as pltpu
from jax.sharding import PartitionSpec as P

QUERY_HEADS = 32
KEY_VALUE_HEADS = 4
HEAD_SIZE = 128
GROUP = QUERY_HEADS // KEY_VALUE_HEADS
THETA = 1000000.0
MESH = pl.DeviceIdType.MESH
BF16 = jnp.bfloat16
F32 = jnp.float32


def kernel(
    owners, members, rows, tile, cap,
    plan_ref, lab_ref, rate_ref, bq_hbm, bk_hbm, bv_hbm, aq_hbm, ak_hbm, av_hbm,
    base_out, actor_out,
    labs, cs, sn, bias, qs, ks, kx, vx, att, land, fwd, bo, out_box, in_box, fin,
    q_sem, k_sem, v_sem,
    lab_send, lab_recv, k_send, v_send, k_recv, v_recv,
    one_send, one_recv, two_send, two_recv, bo_sem, box_send, box_recv, fin_sem,
):
    D = HEAD_SIZE
    me = lax.axis_index("dp")
    s = lax.axis_index("sp")
    back = 2 * rows
    span = 3 * rows
    splits = owners // GROUP
    part = rows // splits

    loads = {}
    for p, q_hbm, k_hbm, v_hbm in ((1, aq_hbm, ak_hbm, av_hbm), (0, bq_hbm, bk_hbm, bv_hbm)):
        loads[p] = (
            pltpu.make_async_copy(q_hbm, qs.at[p], q_sem.at[p]),
            pltpu.make_async_copy(k_hbm, ks.at[p], k_sem.at[p]),
            [
                pltpu.make_async_copy(
                    v_hbm.at[:, pl.ds(h * D, D)], vx.at[p, h, pl.ds(back, rows)], v_sem.at[p, h]
                )
                for h in range(KEY_VALUE_HEADS)
            ],
        )
    for p in (1, 0):
        for load in loads[p][2] + [loads[p][1], loads[p][0]]:
            load.start()

    def col(h):
        return pl.ds(pl.multiple_of(h * D, D), D)

    labs[2] = jnp.broadcast_to(lab_ref[...], labs.shape[1:])
    barrier = pltpu.get_barrier_semaphore()

    def greet_owner(j, c):
        pl.semaphore_signal(
            barrier, inc=1, device_id={"dp": lax.rem(me + j, owners)}, device_id_type=MESH
        )
        return c

    lax.fori_loop(1, owners, greet_owner, 0)
    for j in range(1, members):
        pl.semaphore_signal(
            barrier, inc=1, device_id={"sp": lax.rem(s + j, members)}, device_id_type=MESH
        )
    pl.semaphore_wait(barrier, owners - 1 + members - 1)

    def to_later(src, dst_of, send_sem, recv_sem):
        for step in (1, 2):
            pltpu.make_async_remote_copy(
                src_ref=src,
                dst_ref=dst_of(2 - step),
                send_sem=send_sem,
                recv_sem=recv_sem,
                device_id={"sp": lax.rem(s + step, members)},
                device_id_type=MESH,
            ).start()

    def send_key(p, h):
        to_later(
            kx.at[p, h, pl.ds(back, rows)],
            lambda slot: kx.at[p, h, pl.ds(slot * rows, rows)],
            k_send.at[p], k_recv.at[p, h],
        )

    def send_value(p, h):
        loads[p][2][h].wait()
        to_later(
            vx.at[p, h, pl.ds(back, rows)],
            lambda slot: vx.at[p, h, pl.ds(slot * rows, rows)],
            v_send.at[p], v_recv.at[p, h],
        )

    to_later(labs.at[2], lambda slot: labs.at[slot], lab_send, lab_recv)
    send_value(1, 0)
    pltpu.make_async_copy(labs.at[pl.ds(0, 2)], labs.at[pl.ds(0, 2)], lab_recv).wait()

    lab_row = jnp.concatenate([labs[0, :1, :], labs[1, :1, :], labs[2, :1, :]], axis=1).astype(F32)
    place = lax.broadcasted_iota(jnp.int32, (1, span), 1)
    lab_row = jnp.where(place + (s - 2) * rows >= 0, lab_row, -1.0)
    own = lab_row[:, back:]
    r_id = lax.broadcasted_iota(jnp.int32, (rows, rows), 0)
    c_id = lax.broadcasted_iota(jnp.int32, (rows, rows), 1)
    lab_col = jnp.sum(jnp.where(r_id == c_id, own, 0.0), axis=1, keepdims=True)
    begin = jnp.sum(jnp.where(lab_row < lab_col, 1.0, 0.0), axis=1, keepdims=True)
    r_place = lax.broadcasted_iota(jnp.int32, (rows, 1), 0) + back
    positions = r_place.astype(F32) - begin
    angles = positions * rate_ref[...]
    lane = lax.broadcasted_iota(jnp.int32, (rows, D), 1)
    cs[...] = jnp.cos(angles)
    sine = jnp.sin(angles)
    sn[...] = jnp.where(lane < D // 2, -sine, sine)
    wide = lax.broadcasted_iota(jnp.int32, (rows, span), 1)
    row_of = lax.broadcasted_iota(jnp.int32, (rows, span), 0) + back
    allowed = jnp.where(wide <= row_of, jnp.where(lab_row == lab_col, 0.0, -1e30), -1e30)
    bias[...] = allowed

    def turn(x, r0, n):
        x = x.astype(F32)
        y = x * cs[pl.ds(r0, n), :] + pltpu.roll(x, D // 2, 1) * sn[pl.ds(r0, n), :]
        return y.astype(BF16)

    loads[1][1].wait()
    for h in range(KEY_VALUE_HEADS):
        kx[1, h, back:span, :] = turn(ks[1, :, h * D:(h + 1) * D], 0, rows)
        send_key(1, h)
        if h + 1 < KEY_VALUE_HEADS:
            send_value(1, h + 1)
    loads[0][1].wait()
    for h in range(KEY_VALUE_HEADS):
        kx[0, h, back:span, :] = turn(ks[0, :, h * D:(h + 1) * D], 0, rows)
        send_key(0, h)
        send_value(0, h)
    loads[1][0].wait()

    def arrived(p, h):
        there = kx.at[p, h, pl.ds(0, back)]
        pltpu.make_async_copy(there, there, k_recv.at[p, h]).wait()
        there = vx.at[p, h, pl.ds(0, back)]
        pltpu.make_async_copy(there, there, v_recv.at[p, h]).wait()

    factor = math.log2(math.e) / math.sqrt(D)
    keys = back + tile
    ones = jnp.ones((keys, D), BF16)

    def attend(p, h, head, t):
        q = turn(qs[p, t * tile:(t + 1) * tile, col(head)], t * tile, tile)
        k = kx[p, h, t * tile:t * tile + keys, :]
        v = vx[p, h, t * tile:t * tile + keys, :]
        x = lax.dot_general(q, k, (((1,), (1,)), ((), ())), preferred_element_type=F32)
        x = x * factor + bias[t * tile:(t + 1) * tile, t * tile:t * tile + keys]
        e = jnp.exp2(x - jnp.max(x, axis=1, keepdims=True)).astype(BF16)
        o = jnp.dot(e, jnp.concatenate([v, ones], axis=1), preferred_element_type=F32)
        return (o[:, :D] / o[:, D:]).astype(BF16)

    def move(src, dst, owner, send_sem, recv_sem):
        @pl.when(owner != me)
        def _():
            pltpu.make_async_remote_copy(
                src_ref=src, dst_ref=dst, send_sem=send_sem, recv_sem=recv_sem,
                device_id={"dp": owner}, device_id_type=MESH,
            ).start()

        @pl.when(owner == me)
        def _():
            pltpu.make_async_copy(src, dst, recv_sem).start()

    def drain(ref, sem):
        pltpu.make_async_copy(ref, ref, sem).wait()

    def base_group(h):
        arrived(0, h)

        def two_heads(i, c):
            for k in range(2):
                head = h * GROUP + 2 * i + k
                for t in range(rows // tile):
                    bo[t * tile:(t + 1) * tile, col(head)] = attend(0, h, head, t)
            return c

        lax.fori_loop(0, GROUP // 2, two_heads, 0)
        wide_col = pl.ds(pl.multiple_of(h * GROUP * D, GROUP * D), GROUP * D)
        pltpu.make_async_copy(bo.at[:, wide_col], base_out.at[:, wide_col], bo_sem).start()

    if cap is None:
        def actor_group(h, c):
            arrived(1, h)

            def one_head(i, c):
                j = lax.rem(me // splits + 1 + i, GROUP)
                for t in range(rows // tile):
                    att[h, j, t * tile:(t + 1) * tile, :] = attend(1, h, h * GROUP + j, t)
                for r in range(splits):
                    move(
                        att.at[h, j, pl.ds(r * part, part), :], land.at[h, me], j * splits + r,
                        one_send.at[h], one_recv.at[h],
                    )
                return c

            return lax.fori_loop(0, GROUP, one_head, c)

        my_rows = pl.ds(pl.multiple_of(lax.rem(me, splits) * part, part), part)

        def second_group(h, c):
            base_group(h)
            drain(land.at[h], one_recv.at[h])

            def one_group(i, c):
                g = lax.rem(me + 1 + i, owners)

                def pick(u, val):
                    return jnp.where(plan_ref[u] == g, land[h, u], val)

                fwd[h, g] = lax.fori_loop(1, owners, pick, land[h, 0], unroll=owners <= 8)
                move(
                    fwd.at[h, g], actor_out.at[my_rows, col(h * GROUP + me // splits)], g,
                    two_send.at[h], fin_sem,
                )
                return c

            return lax.fori_loop(0, owners, one_group, c)

        moved = owners - 1
    else:
        half = owners // 2
        per = GROUP // half
        place_of = lax.rem(me, half)
        mine = me - place_of
        other = lax.rem(mine + half, owners)

        def ranks(first):
            taken, groups, out = 0, [], []
            for p in range(half):
                g = plan_ref[first + p]
                near = jnp.where(g >= first, 1, 0) * jnp.where(g < first + half, 1, 0)
                groups.append(g)
                out.append(jnp.where(near == 1, -1, taken))
                taken = taken + 1 - near
            return groups, out

        my_groups, my_ranks = ranks(mine)
        far_groups, far_ranks = ranks(other)

        def actor_piece(h, c):
            arrived(1, h)

            def one_piece(i, c):
                j = lax.rem(place_of + 1 + i, half)
                for k in range(per):
                    for t in range(rows // tile):
                        att[h, j, t * tile:(t + 1) * tile, k * D:(k + 1) * D] = attend(
                            1, h, h * GROUP + j * per + k, t
                        )
                move(att.at[h, j], land.at[h, place_of], mine + j, one_send.at[h], one_recv.at[h])
                return c

            lax.fori_loop(0, half, one_piece, 0)

            @pl.when(h >= 1)
            def _():
                cross(h - 1)

            return c

        def cross(h):
            drain(land.at[h], one_recv.at[h])
            for slot in range(cap):
                val = land[h, 0]
                for p in range(1, half):
                    val = jnp.where(my_ranks[p] == slot, land[h, p], val)
                out_box[h, slot] = val
            pltpu.make_async_remote_copy(
                src_ref=out_box.at[h], dst_ref=in_box.at[h],
                send_sem=box_send.at[h], recv_sem=box_recv.at[h],
                device_id={"dp": lax.rem(me + half, owners)}, device_id_type=MESH,
            ).start()

        wide = per * D
        actor_group = actor_piece

        def second_group(h, c):
            base_group(h)

            @pl.when(h == 0)
            def _():
                cross(KEY_VALUE_HEADS - 1)

            drain(in_box.at[h], box_recv.at[h])

            def one_group(i, c):
                r = lax.rem(place_of + 1 + i, half)
                g = mine + r
                val = land[h, 0]
                for p in range(1, half):
                    val = jnp.where(my_groups[p] == g, land[h, p], val)
                for slot in range(cap):
                    hit = 0
                    for p in range(half):
                        hit = hit + jnp.where(far_groups[p] == g, 1, 0) * jnp.where(
                            far_ranks[p] == slot, 1, 0
                        )
                    val = jnp.where(hit == 1, in_box[h, slot], val)
                fwd[h, r] = val
                move(fwd.at[h, r], fin.at[h, place_of], g, two_send.at[h], two_recv.at[h])
                return c

            return lax.fori_loop(0, half, one_group, c)

        moved = half - 1

    lax.fori_loop(0, KEY_VALUE_HEADS, actor_group, 0)
    loads[0][0].wait()
    lax.fori_loop(0, KEY_VALUE_HEADS, second_group, 0)

    if cap is not None:
        for h in range(KEY_VALUE_HEADS):
            drain(fin.at[h], two_recv.at[h])
            for p in range(half):
                there = pl.ds((h * half + p) * wide, wide)
                pltpu.make_async_copy(fin.at[h, p], actor_out.at[:, there], fin_sem).start()

    drain(labs.at[pl.ds(0, 2)], lab_send)
    for p in range(2):
        drain(kx.at[p, :, pl.ds(0, back), :], k_send.at[p])
        drain(vx.at[p, :, pl.ds(0, back), :], v_send.at[p])
    for h in range(KEY_VALUE_HEADS):
        drain(land.at[h, pl.ds(0, moved)], one_send.at[h])
    drain(base_out, bo_sem)
    for h in range(KEY_VALUE_HEADS):
        drain(land.at[h, pl.ds(0, moved)], two_send.at[h])
        if cap is not None:
            drain(out_box.at[h], box_send.at[h])
    drain(actor_out, fin_sem)


def per_device(owners, members, bq, bk, bv, aq, ak, av, labels, plan):
    rows = bq.shape[1]
    width = bq.shape[2]
    narrow = bk.shape[2]
    D = HEAD_SIZE
    half = np.arange(D) % (D // 2)
    rates = np.exp(half.astype(np.float64) * (-2.0 * math.log(THETA) / D)).astype(np.float32)
    rates = jnp.asarray(rates.reshape(1, D))
    vmem = pl.BlockSpec(memory_space=pltpu.VMEM)
    hbm = pl.BlockSpec(memory_space=pl.ANY)
    out = jax.ShapeDtypeStruct((rows, width), BF16)
    dma = pltpu.SemaphoreType.DMA
    KV = KEY_VALUE_HEADS

    def call(cap, number, *args):
        if cap is None:
            part = (owners, rows // (owners // GROUP), D)
            made = (GROUP, rows, D)
            box = (1, 1, 16, D)
        else:
            part = made = (owners // 2, rows, GROUP // (owners // 2) * D)
            box = (KV, cap) + part[1:]
        return pl.pallas_call(
            functools.partial(kernel, owners, members, rows, rows // 2, cap),
            out_shape=(out, out),
            in_specs=[pl.BlockSpec(memory_space=pltpu.SMEM)] + [vmem] * 2 + [hbm] * 6,
            out_specs=(hbm, hbm),
            scratch_shapes=[
                pltpu.VMEM((3, 8, rows), jnp.int32),
                pltpu.VMEM((rows, D), F32),
                pltpu.VMEM((rows, D), F32),
                pltpu.VMEM((rows, 3 * rows), F32),
                pltpu.VMEM((2, rows, width), BF16),
                pltpu.VMEM((2, rows, narrow), BF16),
                pltpu.VMEM((2, KV, 3 * rows, D), BF16),
                pltpu.VMEM((2, KV, 3 * rows, D), BF16),
                pltpu.VMEM((KV,) + made, BF16),
                pltpu.VMEM((KV,) + part, BF16),
                pltpu.VMEM((KV,) + part, BF16),
                pltpu.VMEM((rows, width), BF16),
                pltpu.VMEM(box, BF16),
                pltpu.VMEM(box, BF16),
                pltpu.VMEM((KV,) + part if cap else (1, 1, 16, D), BF16),
                dma((2,)), dma((2,)), dma((2, KV)),
                dma, dma, dma((2,)), dma((2,)), dma((2, KV)), dma((2, KV)),
                dma((KV,)), dma((KV,)), dma((KV,)), dma((KV,)), dma, dma((KV,)), dma((KV,)), dma,
            ],
            compiler_params=pltpu.CompilerParams(
                collective_id=number, has_side_effects=True, vmem_limit_bytes=60 * 1024 * 1024
            ),
            cost_estimate=pl.CostEstimate(
                flops=2 * 4 * rows * (5 * rows // 2) * width, bytes_accessed=8 * rows * width,
                transcendentals=0,
            ),
        )(*args)

    args = (plan, labels, rates, bq[0], bk[0], bv[0], aq[0], ak[0], av[0])
    if owners != 8:
        base, actor = call(None, 0, *args)
    else:
        leaving = jnp.sum((plan[: owners // 2] >= owners // 2).astype(jnp.int32))
        caps = range(1, owners // 2 + 1)
        base, actor = lax.switch(
            jnp.maximum(leaving, 1) - 1,
            [functools.partial(call, cap, cap) for cap in caps],
            *args,
        )
    return base[None], actor[None]


def solution(mesh):
    rows3 = P("dp", "sp", None)
    return jax.shard_map(
        functools.partial(per_device, mesh.shape["dp"], mesh.shape["sp"]),
        mesh=mesh,
        in_specs=(rows3,) * 6 + (P("dp", "sp"), P()),
        out_specs=(rows3, rows3),
        check_vma=False,
    )
```

```python
import functools
import math

import jax
import jax.numpy as jnp
import numpy as np
from jax import lax
from jax.experimental import pallas as pl
from jax.experimental.pallas import tpu as pltpu
from jax.sharding import PartitionSpec as P

QUERY_HEADS = 32
KEY_VALUE_HEADS = 4
HEAD_SIZE = 128
GROUP = QUERY_HEADS // KEY_VALUE_HEADS
INNER, OUTER = 3, 1
THETA = 1000000.0
MESH = pl.DeviceIdType.MESH
BF16 = jnp.bfloat16
F32 = jnp.float32


def kernel(
    owners, members, rows, tile, cap,
    plan_ref, lab_ref, rate_ref, bq_hbm, bk_hbm, bv_hbm, aq_hbm, ak_hbm, av_hbm,
    base_out, actor_out,
    labs, cs, sn, bias, qs, ks, kx, vx, att, land, fwd, bo, out_box, in_box,
    q_sem, k_sem, v_sem,
    lab_send, lab_recv, k_send, v_send, k_recv, v_recv,
    one_send, one_recv, two_send, two_recv, bo_sem, box_send, box_recv,
):
    D = HEAD_SIZE
    me = lax.axis_index("dp")
    s = lax.axis_index("sp")
    back = 2 * rows
    span = 3 * rows
    splits = owners // GROUP
    part = rows // splits

    loads = {}
    for p, q_hbm, k_hbm, v_hbm in ((1, aq_hbm, ak_hbm, av_hbm), (0, bq_hbm, bk_hbm, bv_hbm)):
        loads[p] = (
            pltpu.make_async_copy(q_hbm, qs.at[p], q_sem.at[p]),
            pltpu.make_async_copy(k_hbm, ks.at[p], k_sem.at[p]),
            pltpu.make_async_copy(v_hbm, vx.at[p, pl.ds(back, rows), :], v_sem.at[p]),
        )
    for p in (1, 0):
        for load in (loads[p][2], loads[p][1], loads[p][0]):
            load.start()

    def col(h):
        return pl.ds(pl.multiple_of(h * D, D), D)

    labs[2] = jnp.broadcast_to(lab_ref[...], labs.shape[1:])
    barrier = pltpu.get_barrier_semaphore()

    def greet_owner(j, c):
        pl.semaphore_signal(
            barrier, inc=1, device_id={"dp": lax.rem(me + j, owners)}, device_id_type=MESH
        )
        return c

    lax.fori_loop(1, owners, greet_owner, 0)
    for j in range(1, members):
        pl.semaphore_signal(
            barrier, inc=1, device_id={"sp": lax.rem(s + j, members)}, device_id_type=MESH
        )
    pl.semaphore_wait(barrier, owners - 1 + members - 1)

    def to_later(src, dst_of, send_sem, recv_sem):
        for step in (1, 2):
            pltpu.make_async_remote_copy(
                src_ref=src,
                dst_ref=dst_of(2 - step),
                send_sem=send_sem,
                recv_sem=recv_sem,
                device_id={"sp": lax.rem(s + step, members)},
                device_id_type=MESH,
            ).start()

    def send_key(p, h):
        to_later(
            kx.at[p, pl.ds(back, rows), col(h)],
            lambda slot: kx.at[p, pl.ds(slot * rows, rows), col(h)],
            k_send.at[p], k_recv.at[p, h],
        )

    def send_value(p, h):
        to_later(
            vx.at[p, pl.ds(back, rows), col(h)],
            lambda slot: vx.at[p, pl.ds(slot * rows, rows), col(h)],
            v_send.at[p], v_recv.at[p, h],
        )

    to_later(labs.at[2], lambda slot: labs.at[slot], lab_send, lab_recv)
    loads[1][2].wait()
    send_value(1, 0)
    pltpu.make_async_copy(labs.at[pl.ds(0, 2)], labs.at[pl.ds(0, 2)], lab_recv).wait()

    lab_row = jnp.concatenate([labs[0, :1, :], labs[1, :1, :], labs[2, :1, :]], axis=1).astype(F32)
    place = lax.broadcasted_iota(jnp.int32, (1, span), 1)
    lab_row = jnp.where(place + (s - 2) * rows >= 0, lab_row, -1.0)
    own = lab_row[:, back:]
    r_id = lax.broadcasted_iota(jnp.int32, (rows, rows), 0)
    c_id = lax.broadcasted_iota(jnp.int32, (rows, rows), 1)
    lab_col = jnp.sum(jnp.where(r_id == c_id, own, 0.0), axis=1, keepdims=True)
    begin = jnp.sum(jnp.where(lab_row < lab_col, 1.0, 0.0), axis=1, keepdims=True)
    r_place = lax.broadcasted_iota(jnp.int32, (rows, 1), 0) + back
    positions = r_place.astype(F32) - begin
    angles = positions * rate_ref[...]
    lane = lax.broadcasted_iota(jnp.int32, (rows, D), 1)
    cs[...] = jnp.cos(angles)
    sine = jnp.sin(angles)
    sn[...] = jnp.where(lane < D // 2, -sine, sine)
    wide = lax.broadcasted_iota(jnp.int32, (rows, span), 1)
    row_of = lax.broadcasted_iota(jnp.int32, (rows, span), 0) + back
    allowed = jnp.where(wide <= row_of, jnp.where(lab_row == lab_col, 0.0, -1e30), -1e30)
    bias[...] = allowed

    def turn(x, r0, n):
        x = x.astype(F32)
        y = x * cs[pl.ds(r0, n), :] + pltpu.roll(x, D // 2, 1) * sn[pl.ds(r0, n), :]
        return y.astype(BF16)

    loads[1][1].wait()
    for h in range(KEY_VALUE_HEADS):
        kx[1, back:span, h * D:(h + 1) * D] = turn(ks[1, :, h * D:(h + 1) * D], 0, rows)
        send_key(1, h)
        if h + 1 < KEY_VALUE_HEADS:
            send_value(1, h + 1)
    loads[0][2].wait()
    loads[0][1].wait()
    for h in range(KEY_VALUE_HEADS):
        kx[0, back:span, h * D:(h + 1) * D] = turn(ks[0, :, h * D:(h + 1) * D], 0, rows)
        send_key(0, h)
        send_value(0, h)
    loads[1][0].wait()

    def arrived(p, h):
        there = kx.at[p, pl.ds(0, back), col(h)]
        pltpu.make_async_copy(there, there, k_recv.at[p, h]).wait()
        there = vx.at[p, pl.ds(0, back), col(h)]
        pltpu.make_async_copy(there, there, v_recv.at[p, h]).wait()

    factor = math.log2(math.e) / math.sqrt(D)
    keys = back + tile
    ones = jnp.ones((keys, D), BF16)

    def attend(p, h, head, t):
        q = turn(qs[p, t * tile:(t + 1) * tile, col(head)], t * tile, tile)
        k = kx[p, t * tile:t * tile + keys, col(h)]
        v = vx[p, t * tile:t * tile + keys, col(h)]
        x = lax.dot_general(q, k, (((1,), (1,)), ((), ())), preferred_element_type=F32)
        x = x * factor + bias[t * tile:(t + 1) * tile, t * tile:t * tile + keys]
        e = jnp.exp2(x - jnp.max(x, axis=1, keepdims=True)).astype(BF16)
        o = jnp.dot(e, jnp.concatenate([v, ones], axis=1), preferred_element_type=F32)
        return (o[:, :D] / o[:, D:]).astype(BF16)

    def move(src, dst, owner, send_sem, recv_sem):
        @pl.when(owner != me)
        def _():
            pltpu.make_async_remote_copy(
                src_ref=src, dst_ref=dst, send_sem=send_sem, recv_sem=recv_sem,
                device_id={"dp": owner}, device_id_type=MESH,
            ).start()

        @pl.when(owner == me)
        def _():
            pltpu.make_async_copy(src, dst, recv_sem).start()

    def drain(ref, sem):
        pltpu.make_async_copy(ref, ref, sem).wait()

    def base_group(h):
        arrived(0, h)

        def two_heads(i, c):
            for k in range(2):
                head = h * GROUP + 2 * i + k
                for t in range(rows // tile):
                    bo[t * tile:(t + 1) * tile, col(head)] = attend(0, h, head, t)
            return c

        lax.fori_loop(0, GROUP // 2, two_heads, 0)
        wide_col = pl.ds(pl.multiple_of(h * GROUP * D, GROUP * D), GROUP * D)
        pltpu.make_async_copy(bo.at[:, wide_col], base_out.at[:, wide_col], bo_sem).start()

    if cap is None:
        def actor_group(h, c):
            arrived(1, h)

            def one_head(i, c):
                j = lax.rem(me // splits + 1 + i, GROUP)
                for t in range(rows // tile):
                    att[h, j, t * tile:(t + 1) * tile, :] = attend(1, h, h * GROUP + j, t)
                for r in range(splits):
                    move(
                        att.at[h, j, pl.ds(r * part, part), :], land.at[h, me], j * splits + r,
                        one_send.at[h], one_recv.at[h],
                    )
                return c

            return lax.fori_loop(0, GROUP, one_head, c)

        my_rows = pl.ds(pl.multiple_of(lax.rem(me, splits) * part, part), part)

        def second_group(h, c):
            base_group(h)
            drain(land.at[h], one_recv.at[h])

            def one_group(i, c):
                g = lax.rem(me + 1 + i, owners)

                def pick(u, val):
                    return jnp.where(plan_ref[u] == g, land[h, u], val)

                fwd[h, g] = lax.fori_loop(1, owners, pick, land[h, 0], unroll=owners <= 8)
                move(
                    fwd.at[h, g], actor_out.at[my_rows, col(h * GROUP + me // splits)], g,
                    two_send.at[h], two_recv,
                )
                return c

            return lax.fori_loop(0, owners, one_group, c)

    else:
        half = owners // 2
        pair = half // 2
        upper = me // half
        mine = upper * half
        other = half - mine
        place = me - mine
        side = lax.rem(place, pair)
        depth = jnp.where(upper == 0, place // pair, 1 - place // pair)
        mirror = other + jnp.where(upper == 0, 1 - depth, depth) * pair + side
        count = jnp.where(depth == 1, INNER, OUTER)
        first = jnp.where(depth == 1, pair * OUTER + side * INNER, side * OUTER)

        def ranks(start):
            taken, groups, out = 0, [], []
            for p in range(half):
                g = plan_ref[start + p]
                near = jnp.where(g >= start, 1, 0) * jnp.where(g < start + half, 1, 0)
                groups.append(g)
                out.append(jnp.where(near == 1, -1, taken))
                taken = taken + 1 - near
            return groups, out

        my_groups, my_ranks = ranks(mine)
        far_groups, far_ranks = ranks(other)

        def actor_piece(h, c):
            arrived(1, h)

            def two_heads(i, c):
                early = pair * OUTER
                low = jnp.where(i == 0, early, jnp.where(i == 1, 0, early + i - 1))
                high = jnp.where(i == 0, early + INNER, jnp.where(i == 1, 1, early + INNER + i - 1))
                for j in (low, high):
                    for t in range(rows // tile):
                        att[h, j, t * tile:(t + 1) * tile, :] = attend(1, h, h * GROUP + j, t)
                for j in (low, high):
                    deep = jnp.where(j >= early, 1, 0)
                    rest = j - deep * early
                    share = jnp.where(deep == 1, INNER, OUTER)
                    line = jnp.where(upper == 0, deep, 1 - deep)
                    turn_of = jnp.where(rest >= share, 1, 0)
                    unit = rest - turn_of * share
                    move(
                        att.at[h, j], land.at[h, unit, place],
                        mine + line * pair + turn_of,
                        one_send.at[h], one_recv.at[h, unit],
                    )
                return c

            lax.fori_loop(0, GROUP // 2, two_heads, 0)

            @pl.when(h == KEY_VALUE_HEADS - 1)
            def _():
                loads[0][0].wait()
                base_group(0)

            cross(h)

            @pl.when(h >= 1)
            def _():
                outward(h - 1)

            return c

        def cross(h):
            def unit(k, c):
                drain(land.at[h, k], one_recv.at[h, k])
                for slot in range(cap):
                    val = land[h, k, 0]
                    for p in range(1, half):
                        val = jnp.where(my_ranks[p] == slot, land[h, k, p], val)
                    out_box[h, k, slot] = val
                pltpu.make_async_remote_copy(
                    src_ref=out_box.at[h, k], dst_ref=in_box.at[h, k],
                    send_sem=box_send.at[h, k], recv_sem=box_recv.at[h, k],
                    device_id={"dp": mirror}, device_id_type=MESH,
                ).start()
                return c

            lax.fori_loop(0, count, unit, 0)

        actor_group = actor_piece

        def second_group(h, c):
            @pl.when(h == KEY_VALUE_HEADS - 1)
            def _():
                outward(h)

            base_group(h)
            return c

        def outward(h):
            def unit(k, c):
                drain(in_box.at[h, k], box_recv.at[h, k])

                def one_group(i, c):
                    r = lax.rem(place + 1 + i, half)
                    g = mine + r
                    val = land[h, k, 0]
                    for p in range(1, half):
                        val = jnp.where(my_groups[p] == g, land[h, k, p], val)
                    for slot in range(cap):
                        hit = 0
                        for p in range(half):
                            hit = hit + jnp.where(far_groups[p] == g, 1, 0) * jnp.where(
                                far_ranks[p] == slot, 1, 0
                            )
                        val = jnp.where(hit == 1, in_box[h, k, slot], val)
                    fwd[h, k, r] = val
                    move(
                        fwd.at[h, k, r], actor_out.at[:, col(h * GROUP + first + k)], g,
                        two_send.at[h, k], two_recv,
                    )
                    return c

                return lax.fori_loop(0, half, one_group, c)

            lax.fori_loop(0, count, unit, 0)

    lax.fori_loop(0, KEY_VALUE_HEADS, actor_group, 0)
    if cap is None:
        loads[0][0].wait()
    lax.fori_loop(0 if cap is None else 1, KEY_VALUE_HEADS, second_group, 0)

    drain(labs.at[pl.ds(0, 2)], lab_send)
    for p in range(2):
        drain(kx.at[p, pl.ds(0, back), :], k_send.at[p])
        drain(vx.at[p, pl.ds(0, back), :], v_send.at[p])
    drain(base_out, bo_sem)
    for h in range(KEY_VALUE_HEADS):
        if cap is None:
            drain(land.at[h, pl.ds(0, owners - 1)], one_send.at[h])
            drain(land.at[h, pl.ds(0, owners - 1)], two_send.at[h])
        else:
            for kind, share in enumerate((OUTER, INNER)):
                @pl.when(depth == kind)
                def _():
                    drain(att.at[h, pl.ds(0, GROUP - share)], one_send.at[h])
                    for k in range(share):
                        drain(out_box.at[h, k], box_send.at[h, k])
                        drain(fwd.at[h, k, pl.ds(0, half - 1)], two_send.at[h, k])
    drain(actor_out, two_recv)


def per_device(owners, members, bq, bk, bv, aq, ak, av, labels, plan):
    rows = bq.shape[1]
    width = bq.shape[2]
    narrow = bk.shape[2]
    D = HEAD_SIZE
    half = np.arange(D) % (D // 2)
    rates = np.exp(half.astype(np.float64) * (-2.0 * math.log(THETA) / D)).astype(np.float32)
    rates = jnp.asarray(rates.reshape(1, D))
    vmem = pl.BlockSpec(memory_space=pltpu.VMEM)
    hbm = pl.BlockSpec(memory_space=pl.ANY)
    out = jax.ShapeDtypeStruct((rows, width), BF16)
    dma = pltpu.SemaphoreType.DMA
    KV = KEY_VALUE_HEADS

    def call(cap, number, *args):
        if cap is None:
            part = (owners, rows // (owners // GROUP), D)
            box = (1, 1, 16, D)
            sems = (KV,)
        else:
            part = (INNER, owners // 2, rows, D)
            box = (KV, INNER, cap, rows, D)
            sems = (KV, INNER)
        return pl.pallas_call(
            functools.partial(kernel, owners, members, rows, rows // 2, cap),
            out_shape=(out, out),
            in_specs=[pl.BlockSpec(memory_space=pltpu.SMEM)] + [vmem] * 2 + [hbm] * 6,
            out_specs=(hbm, hbm),
            scratch_shapes=[
                pltpu.VMEM((3, 8, rows), jnp.int32),
                pltpu.VMEM((rows, D), F32),
                pltpu.VMEM((rows, D), F32),
                pltpu.VMEM((rows, 3 * rows), F32),
                pltpu.VMEM((2, rows, width), BF16),
                pltpu.VMEM((2, rows, narrow), BF16),
                pltpu.VMEM((2, 3 * rows, narrow), BF16),
                pltpu.VMEM((2, 3 * rows, narrow), BF16),
                pltpu.VMEM((KV, GROUP, rows, D), BF16),
                pltpu.VMEM((KV,) + part, BF16),
                pltpu.VMEM((KV,) + part, BF16),
                pltpu.VMEM((rows, width), BF16),
                pltpu.VMEM(box, BF16),
                pltpu.VMEM(box, BF16),
                dma((2,)), dma((2,)), dma((2,)),
                dma, dma, dma((2,)), dma((2,)), dma((2, KV)), dma((2, KV)),
                dma((KV,)), dma(sems), dma(sems), dma, dma, dma(sems), dma(sems),
            ],
            compiler_params=pltpu.CompilerParams(
                collective_id=number, has_side_effects=True, vmem_limit_bytes=60 * 1024 * 1024
            ),
            cost_estimate=pl.CostEstimate(
                flops=2 * 4 * rows * (5 * rows // 2) * width, bytes_accessed=8 * rows * width,
                transcendentals=0,
            ),
        )(*args)

    args = (plan, labels, rates, bq[0], bk[0], bv[0], aq[0], ak[0], av[0])
    if owners != 8:
        base, actor = call(None, 0, *args)
    else:
        leaving = jnp.sum((plan[: owners // 2] >= owners // 2).astype(jnp.int32))
        caps = range(1, owners // 2 + 1)
        base, actor = lax.switch(
            jnp.maximum(leaving, 1) - 1,
            [functools.partial(call, cap, cap) for cap in caps],
            *args,
        )
    return base[None], actor[None]


def solution(mesh):
    rows3 = P("dp", "sp", None)
    return jax.shard_map(
        functools.partial(per_device, mesh.shape["dp"], mesh.shape["sp"]),
        mesh=mesh,
        in_specs=(rows3,) * 6 + (P("dp", "sp"), P()),
        out_specs=(rows3, rows3),
        check_vma=False,
    )
```

```python
import functools
import math

import jax
import jax.numpy as jnp
import numpy as np
from jax import lax
from jax.experimental import pallas as pl
from jax.experimental.pallas import tpu as pltpu
from jax.sharding import PartitionSpec as P

QUERY_HEADS = 32
KEY_VALUE_HEADS = 4
HEAD_SIZE = 128
GROUP = QUERY_HEADS // KEY_VALUE_HEADS
INNER, OUTER = 3, 1
THETA = 1000000.0
MESH = pl.DeviceIdType.MESH
BF16 = jnp.bfloat16
F32 = jnp.float32


def kernel(
    owners, members, rows, tile, cap,
    plan_ref, lab_ref, rate_ref, bq_hbm, bk_hbm, bv_hbm, aq_hbm, ak_hbm, av_hbm,
    base_out, actor_out,
    labs, cs, sn, bias, qs, ks, kx, vx, att, land, fwd, bo, out_box, in_box,
    q_sem, k_sem, v_sem,
    lab_send, lab_recv, k_send, v_send, k_recv, v_recv,
    one_send, one_recv, two_send, two_recv, bo_sem, box_send, box_recv,
):
    D = HEAD_SIZE
    me = lax.axis_index("dp")
    s = lax.axis_index("sp")
    back = 2 * rows
    span = 3 * rows
    splits = owners // GROUP
    part = rows // splits

    loads = {}
    for p, q_hbm, k_hbm, v_hbm in ((1, aq_hbm, ak_hbm, av_hbm), (0, bq_hbm, bk_hbm, bv_hbm)):
        loads[p] = (
            pltpu.make_async_copy(q_hbm, qs.at[p], q_sem.at[p]),
            pltpu.make_async_copy(k_hbm, ks.at[p], k_sem.at[p]),
            pltpu.make_async_copy(v_hbm, vx.at[p, pl.ds(back, rows), :], v_sem.at[p]),
        )
    for p in (1, 0):
        for load in (loads[p][2], loads[p][1], loads[p][0]):
            load.start()

    def col(h):
        return pl.ds(pl.multiple_of(h * D, D), D)

    labs[2] = jnp.broadcast_to(lab_ref[...], labs.shape[1:])
    barrier = pltpu.get_barrier_semaphore()

    def greet_owner(j, c):
        pl.semaphore_signal(
            barrier, inc=1, device_id={"dp": lax.rem(me + j, owners)}, device_id_type=MESH
        )
        return c

    lax.fori_loop(1, owners, greet_owner, 0)
    for j in range(1, members):
        pl.semaphore_signal(
            barrier, inc=1, device_id={"sp": lax.rem(s + j, members)}, device_id_type=MESH
        )
    pl.semaphore_wait(barrier, owners - 1 + members - 1)

    def to_later(src, dst_of, send_sem, recv_sem):
        for step in (1, 2):
            pltpu.make_async_remote_copy(
                src_ref=src,
                dst_ref=dst_of(2 - step),
                send_sem=send_sem,
                recv_sem=recv_sem,
                device_id={"sp": lax.rem(s + step, members)},
                device_id_type=MESH,
            ).start()

    def send_key(p, h):
        to_later(
            kx.at[p, pl.ds(back, rows), col(h)],
            lambda slot: kx.at[p, pl.ds(slot * rows, rows), col(h)],
            k_send.at[p], k_recv.at[p, h],
        )

    def send_value(p, h):
        to_later(
            vx.at[p, pl.ds(back, rows), col(h)],
            lambda slot: vx.at[p, pl.ds(slot * rows, rows), col(h)],
            v_send.at[p], v_recv.at[p, h],
        )

    to_later(labs.at[2], lambda slot: labs.at[slot], lab_send, lab_recv)
    loads[1][2].wait()
    send_value(1, 0)
    pltpu.make_async_copy(labs.at[pl.ds(0, 2)], labs.at[pl.ds(0, 2)], lab_recv).wait()

    lab_row = jnp.concatenate([labs[0, :1, :], labs[1, :1, :], labs[2, :1, :]], axis=1).astype(F32)
    place = lax.broadcasted_iota(jnp.int32, (1, span), 1)
    lab_row = jnp.where(place + (s - 2) * rows >= 0, lab_row, -1.0)
    own = lab_row[:, back:]
    r_id = lax.broadcasted_iota(jnp.int32, (rows, rows), 0)
    c_id = lax.broadcasted_iota(jnp.int32, (rows, rows), 1)
    lab_col = jnp.sum(jnp.where(r_id == c_id, own, 0.0), axis=1, keepdims=True)
    begin = jnp.sum(jnp.where(lab_row < lab_col, 1.0, 0.0), axis=1, keepdims=True)
    r_place = lax.broadcasted_iota(jnp.int32, (rows, 1), 0) + back
    positions = r_place.astype(F32) - begin
    angles = positions * rate_ref[...]
    lane = lax.broadcasted_iota(jnp.int32, (rows, D), 1)
    cs[...] = jnp.cos(angles)
    sine = jnp.sin(angles)
    sn[...] = jnp.where(lane < D // 2, -sine, sine)
    wide = lax.broadcasted_iota(jnp.int32, (rows, span), 1)
    row_of = lax.broadcasted_iota(jnp.int32, (rows, span), 0) + back
    allowed = jnp.where(wide <= row_of, jnp.where(lab_row == lab_col, 0.0, -1e30), -1e30)
    bias[...] = allowed

    def turn(x, r0, n):
        x = x.astype(F32)
        y = x * cs[pl.ds(r0, n), :] + pltpu.roll(x, D // 2, 1) * sn[pl.ds(r0, n), :]
        return y.astype(BF16)

    loads[1][1].wait()
    for h in range(KEY_VALUE_HEADS):
        kx[1, back:span, h * D:(h + 1) * D] = turn(ks[1, :, h * D:(h + 1) * D], 0, rows)
        send_key(1, h)
        if h + 1 < KEY_VALUE_HEADS:
            send_value(1, h + 1)
    def send_base():
        loads[0][2].wait()
        loads[0][1].wait()
        for h in range(KEY_VALUE_HEADS):
            kx[0, back:span, h * D:(h + 1) * D] = turn(ks[0, :, h * D:(h + 1) * D], 0, rows)
            send_key(0, h)
            send_value(0, h)

    if cap is None:
        send_base()
    loads[1][0].wait()

    def arrived(p, h):
        there = kx.at[p, pl.ds(0, back), col(h)]
        pltpu.make_async_copy(there, there, k_recv.at[p, h]).wait()
        there = vx.at[p, pl.ds(0, back), col(h)]
        pltpu.make_async_copy(there, there, v_recv.at[p, h]).wait()

    factor = math.log2(math.e) / math.sqrt(D)
    keys = back + tile
    ones = jnp.ones((keys, D), BF16)

    def attend(p, h, head, t):
        q = turn(qs[p, t * tile:(t + 1) * tile, col(head)], t * tile, tile)
        k = kx[p, t * tile:t * tile + keys, col(h)]
        v = vx[p, t * tile:t * tile + keys, col(h)]
        x = lax.dot_general(q, k, (((1,), (1,)), ((), ())), preferred_element_type=F32)
        x = x * factor + bias[t * tile:(t + 1) * tile, t * tile:t * tile + keys]
        e = jnp.exp2(x - jnp.max(x, axis=1, keepdims=True)).astype(BF16)
        o = jnp.dot(e, jnp.concatenate([v, ones], axis=1), preferred_element_type=F32)
        return (o[:, :D] / o[:, D:]).astype(BF16)

    def move(src, dst, owner, send_sem, recv_sem):
        @pl.when(owner != me)
        def _():
            pltpu.make_async_remote_copy(
                src_ref=src, dst_ref=dst, send_sem=send_sem, recv_sem=recv_sem,
                device_id={"dp": owner}, device_id_type=MESH,
            ).start()

        @pl.when(owner == me)
        def _():
            pltpu.make_async_copy(src, dst, recv_sem).start()

    def drain(ref, sem):
        pltpu.make_async_copy(ref, ref, sem).wait()

    def base_group(h):
        arrived(0, h)

        def two_heads(i, c):
            for k in range(2):
                head = h * GROUP + 2 * i + k
                for t in range(rows // tile):
                    bo[t * tile:(t + 1) * tile, col(head)] = attend(0, h, head, t)
            return c

        lax.fori_loop(0, GROUP // 2, two_heads, 0)
        wide_col = pl.ds(pl.multiple_of(h * GROUP * D, GROUP * D), GROUP * D)
        pltpu.make_async_copy(bo.at[:, wide_col], base_out.at[:, wide_col], bo_sem).start()

    if cap is None:
        def actor_group(h, c):
            arrived(1, h)

            def one_head(i, c):
                j = lax.rem(me // splits + 1 + i, GROUP)
                for t in range(rows // tile):
                    att[h, j, t * tile:(t + 1) * tile, :] = attend(1, h, h * GROUP + j, t)
                for r in range(splits):
                    move(
                        att.at[h, j, pl.ds(r * part, part), :], land.at[h, me], j * splits + r,
                        one_send.at[h], one_recv.at[h],
                    )
                return c

            return lax.fori_loop(0, GROUP, one_head, c)

        my_rows = pl.ds(pl.multiple_of(lax.rem(me, splits) * part, part), part)

        def second_group(h, c):
            base_group(h)
            drain(land.at[h], one_recv.at[h])

            def one_group(i, c):
                g = lax.rem(me + 1 + i, owners)

                def pick(u, val):
                    return jnp.where(plan_ref[u] == g, land[h, u], val)

                fwd[h, g] = lax.fori_loop(1, owners, pick, land[h, 0], unroll=owners <= 8)
                move(
                    fwd.at[h, g], actor_out.at[my_rows, col(h * GROUP + me // splits)], g,
                    two_send.at[h], two_recv,
                )
                return c

            return lax.fori_loop(0, owners, one_group, c)

    else:
        half = owners // 2
        pair = half // 2
        upper = me // half
        mine = upper * half
        other = half - mine
        place = me - mine
        side = lax.rem(place, pair)
        depth = jnp.where(upper == 0, place // pair, 1 - place // pair)
        mirror = other + jnp.where(upper == 0, 1 - depth, depth) * pair + side
        count = jnp.where(depth == 1, INNER, OUTER)
        first = jnp.where(depth == 1, pair * OUTER + side * INNER, side * OUTER)

        def ranks(start):
            taken, groups, out = 0, [], []
            for p in range(half):
                g = plan_ref[start + p]
                near = jnp.where(g >= start, 1, 0) * jnp.where(g < start + half, 1, 0)
                groups.append(g)
                out.append(jnp.where(near == 1, -1, taken))
                taken = taken + 1 - near
            return groups, out

        my_groups, my_ranks = ranks(mine)
        far_groups, far_ranks = ranks(other)

        def actor_piece(h, c):
            arrived(1, h)

            def two_heads(i, c):
                early = pair * OUTER
                low = jnp.where(i == 0, early, jnp.where(i == 1, 0, early + i - 1))
                high = jnp.where(i == 0, early + INNER, jnp.where(i == 1, 1, early + INNER + i - 1))
                for j in (low, high):
                    for t in range(rows // tile):
                        att[h, j, t * tile:(t + 1) * tile, :] = attend(1, h, h * GROUP + j, t)
                for j in (low, high):
                    deep = jnp.where(j >= early, 1, 0)
                    rest = j - deep * early
                    share = jnp.where(deep == 1, INNER, OUTER)
                    line = jnp.where(upper == 0, deep, 1 - deep)
                    turn_of = jnp.where(rest >= share, 1, 0)
                    unit = rest - turn_of * share
                    move(
                        att.at[h, j], land.at[h, unit, place],
                        mine + line * pair + turn_of,
                        one_send.at[h], one_recv.at[h, unit],
                    )
                return c

            lax.fori_loop(0, GROUP // 2, two_heads, 0)

            @pl.when(h == 0)
            def _():
                send_base()

            @pl.when(h == KEY_VALUE_HEADS - 1)
            def _():
                loads[0][0].wait()
                base_group(0)

            cross(h)

            @pl.when(h >= 1)
            def _():
                outward(h - 1)

            return c

        def cross(h):
            def unit(k, c):
                drain(land.at[h, k], one_recv.at[h, k])
                for slot in range(cap):
                    val = land[h, k, 0]
                    for p in range(1, half):
                        val = jnp.where(my_ranks[p] == slot, land[h, k, p], val)
                    out_box[h, k, slot] = val
                pltpu.make_async_remote_copy(
                    src_ref=out_box.at[h, k], dst_ref=in_box.at[h, k],
                    send_sem=box_send.at[h, k], recv_sem=box_recv.at[h, k],
                    device_id={"dp": mirror}, device_id_type=MESH,
                ).start()
                return c

            lax.fori_loop(0, count, unit, 0)

        actor_group = actor_piece

        def second_group(h, c):
            @pl.when(h == KEY_VALUE_HEADS - 2)
            def _():
                outward(h + 1)

            base_group(h)
            return c

        def outward(h):
            def unit(k, c):
                drain(in_box.at[h, k], box_recv.at[h, k])

                def one_group(i, c):
                    r = lax.rem(place + 1 + i, half)
                    g = mine + r
                    val = land[h, k, 0]
                    for p in range(1, half):
                        val = jnp.where(my_groups[p] == g, land[h, k, p], val)
                    for slot in range(cap):
                        hit = 0
                        for p in range(half):
                            hit = hit + jnp.where(far_groups[p] == g, 1, 0) * jnp.where(
                                far_ranks[p] == slot, 1, 0
                            )
                        val = jnp.where(hit == 1, in_box[h, k, slot], val)
                    fwd[h, k, r] = val
                    move(
                        fwd.at[h, k, r], actor_out.at[:, col(h * GROUP + first + k)], g,
                        two_send.at[h, k], two_recv,
                    )
                    return c

                return lax.fori_loop(0, half, one_group, c)

            lax.fori_loop(0, count, unit, 0)

    lax.fori_loop(0, KEY_VALUE_HEADS, actor_group, 0)
    if cap is None:
        loads[0][0].wait()
    lax.fori_loop(0 if cap is None else 1, KEY_VALUE_HEADS, second_group, 0)

    drain(labs.at[pl.ds(0, 2)], lab_send)
    for p in range(2):
        drain(kx.at[p, pl.ds(0, back), :], k_send.at[p])
        drain(vx.at[p, pl.ds(0, back), :], v_send.at[p])
    drain(base_out, bo_sem)
    for h in range(KEY_VALUE_HEADS):
        if cap is None:
            drain(land.at[h, pl.ds(0, owners - 1)], one_send.at[h])
            drain(land.at[h, pl.ds(0, owners - 1)], two_send.at[h])
        else:
            for kind, share in enumerate((OUTER, INNER)):
                @pl.when(depth == kind)
                def _():
                    drain(att.at[h, pl.ds(0, GROUP - share)], one_send.at[h])
                    for k in range(share):
                        drain(out_box.at[h, k], box_send.at[h, k])
                        drain(fwd.at[h, k, pl.ds(0, half - 1)], two_send.at[h, k])
    drain(actor_out, two_recv)


def per_device(owners, members, bq, bk, bv, aq, ak, av, labels, plan):
    rows = bq.shape[1]
    width = bq.shape[2]
    narrow = bk.shape[2]
    D = HEAD_SIZE
    half = np.arange(D) % (D // 2)
    rates = np.exp(half.astype(np.float64) * (-2.0 * math.log(THETA) / D)).astype(np.float32)
    rates = jnp.asarray(rates.reshape(1, D))
    vmem = pl.BlockSpec(memory_space=pltpu.VMEM)
    hbm = pl.BlockSpec(memory_space=pl.ANY)
    out = jax.ShapeDtypeStruct((rows, width), BF16)
    dma = pltpu.SemaphoreType.DMA
    KV = KEY_VALUE_HEADS

    def call(cap, number, *args):
        if cap is None:
            part = (owners, rows // (owners // GROUP), D)
            box = (1, 1, 16, D)
            sems = (KV,)
        else:
            part = (INNER, owners // 2, rows, D)
            box = (KV, INNER, cap, rows, D)
            sems = (KV, INNER)
        return pl.pallas_call(
            functools.partial(kernel, owners, members, rows, rows // 2, cap),
            out_shape=(out, out),
            in_specs=[pl.BlockSpec(memory_space=pltpu.SMEM)] + [vmem] * 2 + [hbm] * 6,
            out_specs=(hbm, hbm),
            scratch_shapes=[
                pltpu.VMEM((3, 8, rows), jnp.int32),
                pltpu.VMEM((rows, D), F32),
                pltpu.VMEM((rows, D), F32),
                pltpu.VMEM((rows, 3 * rows), F32),
                pltpu.VMEM((2, rows, width), BF16),
                pltpu.VMEM((2, rows, narrow), BF16),
                pltpu.VMEM((2, 3 * rows, narrow), BF16),
                pltpu.VMEM((2, 3 * rows, narrow), BF16),
                pltpu.VMEM((KV, GROUP, rows, D), BF16),
                pltpu.VMEM((KV,) + part, BF16),
                pltpu.VMEM((KV,) + part, BF16),
                pltpu.VMEM((rows, width), BF16),
                pltpu.VMEM(box, BF16),
                pltpu.VMEM(box, BF16),
                dma((2,)), dma((2,)), dma((2,)),
                dma, dma, dma((2,)), dma((2,)), dma((2, KV)), dma((2, KV)),
                dma((KV,)), dma(sems), dma(sems), dma, dma, dma(sems), dma(sems),
            ],
            compiler_params=pltpu.CompilerParams(
                collective_id=number, has_side_effects=True, vmem_limit_bytes=60 * 1024 * 1024
            ),
            cost_estimate=pl.CostEstimate(
                flops=2 * 4 * rows * (5 * rows // 2) * width, bytes_accessed=8 * rows * width,
                transcendentals=0,
            ),
        )(*args)

    args = (plan, labels, rates, bq[0], bk[0], bv[0], aq[0], ak[0], av[0])
    if owners != 8:
        base, actor = call(None, 0, *args)
    else:
        leaving = jnp.sum((plan[: owners // 2] >= owners // 2).astype(jnp.int32))
        caps = range(1, owners // 2 + 1)
        base, actor = lax.switch(
            jnp.maximum(leaving, 1) - 1,
            [functools.partial(call, cap, cap) for cap in caps],
            *args,
        )
    return base[None], actor[None]


def solution(mesh):
    rows3 = P("dp", "sp", None)
    return jax.shard_map(
        functools.partial(per_device, mesh.shape["dp"], mesh.shape["sp"]),
        mesh=mesh,
        in_specs=(rows3,) * 6 + (P("dp", "sp"), P()),
        out_specs=(rows3, rows3),
        check_vma=False,
    )
```
